256 devices in a mesh: seq: 16 (over z, core), fsdp: 16 (over y, x).
Axes of the slice: x: 4, y: 4, z: 8, core: 2. Of those that a mesh axis runs over, the one named last changes fastest.
Arguments:
- queries: bfloat16 [3, 16384, 4096], P(None, 'seq', 'fsdp'), may hold values from -6 to 6
- keys: bfloat16 [3, 16384, 4096], P(None, 'seq', 'fsdp'), may hold values from -6 to 6
- values: bfloat16 [3, 16384, 4096], P(None, 'seq', 'fsdp'), may hold values from -6 to 6
- out_grad: bfloat16 [3, 16384, 4096], P(None, 'seq', 'fsdp'), may hold values from -6 to 6
- gain: float32 [3, 4096], P(None, 'fsdp'), may hold values from 0.5 to 1.5
- keep_mask: int32 [3], replicated, may hold values from 0 to 1, as said below
- segments: int32 [16384], P('seq'), may hold values from 0 to 3, never falling along the last dimension, each value on 1 to 8192 neighbouring positions
Outputs:
- query_grad: bfloat16 [3, 16384, 4096], P(None, 'seq', 'fsdp')
- key_grad: bfloat16 [3, 16384, 4096], P(None, 'seq', 'fsdp')
- value_grad: bfloat16 [3, 16384, 4096], P(None, 'seq', 'fsdp')
- gain_grad: float32 [3, 4096], P(None, 'fsdp')
The draws below stay inside these ranges and needn't reach their ends.
Inputs may be any that keep to these rules, and one draw needn't show every extreme that they name: `segments`: segment numbers never fall along the sequence; a document has 1 to 8192 tokens. `keep_mask`: at least one layer is kept.
All inputs are finite; a program needn't handle non-finite values.
Results may differ from the reference program's by a relative error of at most 0.0058.
Values sent between devices are 32-bit elements; how exact they have to be, the bound alone decides.
A program may use at most 128 MiB of HBM per device.

```python
import math
import jax
import jax.numpy as jnp
import numpy as np
from jax import lax

DH = 128
H = 32
LAYERS = 3
BLK = 512
TOKENS = 16384


def draw_keep_mask(key, part):
    key = jax.random.fold_in(key, 7)
    pattern = jax.random.randint(key, (), 1, 2 ** LAYERS, dtype=jnp.int32)
    places = jnp.arange(LAYERS, dtype=jnp.int32)
    return jnp.bitwise_and(jnp.right_shift(pattern, places), 1).astype(jnp.int32)


def steps_of(rng, dims, cuts, smallest, high):
    loudness, own = 1.0, jax.random.fold_in(rng, 6)
    for dim, shards_of in cuts:
        heights = jnp.exp(jax.random.uniform(jax.random.fold_in(own, dim), (shards_of,), jnp.float32, smallest / len(cuts), high / len(cuts)))
        loudness = loudness * jnp.repeat(heights, dims[dim] // shards_of).reshape([-1 if axis == dim else 1 for axis in range(len(dims))])
    return loudness


def profile(count, total, most, skew):
    loads = [(1 << 20) // math.isqrt(grade ** skew) + 1 for grade in range(2, count + 1)]
    spare, counts = total - most - (count - 1), [1] * (count - 1)
    while spare > 0:
        candidates = [i for i in range(count - 1) if counts[i] < most]
        whole, remaining = sum([loads[i] for i in candidates]), spare
        for i in candidates:
            extra = min(most - counts[i], max(1, remaining * loads[i] // whole), spare)
            counts[i] = counts[i] + extra
            spare = spare - extra
    return np.array([most] + counts)


def ragged_sizes(rng, count, total, reach, lean):
    if count == 2:
        one = jax.random.randint(rng, (), max(1, total - reach), min(reach, total - 1) + 1)
        return jnp.stack([one, total - one])
    lengths = jnp.asarray(profile(count, total, reach, lean), jnp.int32)
    twos = (count - 1) // 2
    giver, receiver = lengths[1:1 + 2 * twos:2], lengths[2:2 + 2 * twos:2]
    room = jnp.minimum(giver - 1, reach - receiver)
    moved = jax.random.randint(jax.random.fold_in(rng, 1), (twos,), 0, 1 << 20) % (room + 1)
    lengths = lengths.at[1:1 + 2 * twos:2].set(giver - moved).at[2:2 + 2 * twos:2].set(receiver + moved)
    return lengths[jax.random.permutation(jax.random.fold_in(rng, 2), count)]


def centred(rng, extent, deviation, limit, cuts=(), kind=jnp.bfloat16):
    loudness = steps_of(rng, extent, cuts, -0.22, 0.18) if cuts else 1.0
    entries = jax.random.normal(rng, extent, jnp.float32) * deviation * loudness
    return jnp.minimum(jnp.maximum(entries, -limit), limit).astype(kind)


def setup_inputs(seed: int = 0) -> dict:
    splits = jax.random.split(jax.random.key(seed), 8)
    queries = centred(splits[0], (LAYERS, TOKENS, H * DH), 1.0, 6.0, ((1, 16), (2, 16)))
    keys = centred(splits[1], (LAYERS, TOKENS, H * DH), 1.0, 6.0, ((1, 16), (2, 16)))
    values = centred(splits[2], (LAYERS, TOKENS, H * DH), 1.0, 6.0, ((1, 16), (2, 16)))
    out_grad = centred(splits[3], (LAYERS, TOKENS, H * DH), 1.0, 6.0, ((1, 16), (2, 16)))
    gain = jnp.clip(0.5 + 1.0 * jax.random.uniform(splits[4], (LAYERS, H * DH), jnp.float32) ** steps_of(splits[4], (LAYERS, H * DH), ((1, 16),), -0.2, 0.2), 0.5, 1.5)
    keep_mask = draw_keep_mask(jax.random.fold_in(splits[7], 71), 0)
    segments = jnp.searchsorted(jnp.cumsum(ragged_sizes(splits[6], 4, TOKENS, TOKENS // 2, 0)), jnp.arange(TOKENS), side="right").astype(jnp.int32)
    return dict(queries=queries, keys=keys, values=values, out_grad=out_grad, gain=gain, keep_mask=keep_mask, segments=segments)


HIGH = lax.Precision.HIGHEST
EPSILON = 1e-06
KEEP_RATE = 0.75

def join_states(first_part, second_part):
    seg_first, state_first = first_part
    seg_second, state_second = second_part
    empty = seg_second < 0
    carried = jnp.logical_or(seg_second == seg_first, empty)
    return (jnp.where(empty, seg_first, seg_second), state_second + jnp.where(carried, state_first, jnp.float32(0.0)))

def running_states(summaries, summary_segs, backward):
    opening = (jnp.float32(-1.0), jnp.zeros(summaries.shape[1:], jnp.float32))

    def advance(carry, inputs):
        return (join_states(carry, inputs), carry)
    final, before = lax.scan(advance, opening, (summary_segs, summaries), reverse=backward)
    return before

def to_bf16_and_back(array):
    return lax.optimization_barrier(array.astype(jnp.bfloat16)).astype(jnp.float32)

def reference(queries, keys, values, out_grad, gain, keep_mask, segments):
    block_count = TOKENS // BLK
    feature_count = H * DH
    seg_values = segments.astype(jnp.float32).reshape(block_count, BLK)
    places = jnp.arange(BLK)
    causal = places[:, None] >= places[None, :]
    within = jnp.logical_and(causal[None], seg_values[:, :, None] == seg_values[:, None, :])
    tail_select = seg_values == seg_values[:, -1:]
    head_select = seg_values == seg_values[:, :1]
    grads_query, grads_key, grads_value, grads_gain = ([], [], [], [])
    for layer in range(LAYERS):
        query_blocks = queries[layer].astype(jnp.float32).reshape(block_count, BLK, H, DH)
        key_blocks = keys[layer].astype(jnp.float32).reshape(block_count, BLK, H, DH)
        value_blocks = values[layer].astype(jnp.float32).reshape(block_count, BLK, H, DH)
        tails = jnp.einsum('bshd,bshe->bhde', jnp.where(tail_select[:, :, None, None], key_blocks, 0.0), value_blocks, precision=HIGH)
        fwd_segs, fwd_states = running_states(tails, seg_values[:, -1], False)
        seen_fwd = seg_values == fwd_segs[:, None]

        def forward_block(pieces):
            query_one, key_one, value_one, mask_one, seen_one, state_one = pieces
            scores = jnp.einsum('thd,shd->hts', query_one, key_one, precision=HIGH)
            weights = to_bf16_and_back(jnp.where(mask_one[None], scores, 0.0))
            carried = jnp.einsum('thd,hde->the', query_one, to_bf16_and_back(state_one), precision=HIGH)
            inner = jnp.einsum('hts,shd->thd', weights, value_one, precision=HIGH)
            return inner + jnp.where(seen_one[:, None, None], carried, 0.0)
        attention = lax.map(forward_block, (query_blocks, key_blocks, value_blocks, within, seen_fwd, fwd_states))
        attention = attention.reshape(TOKENS, feature_count)
        keep_scale = keep_mask[layer].astype(jnp.float32) / KEEP_RATE
        upstream = out_grad[layer].astype(jnp.float32)
        weighted = upstream * gain[layer][None, :]
        inverse = 1.0 / jnp.sqrt(lax.optimization_barrier(jnp.mean(attention * attention, -1)) + EPSILON)
        cross = lax.optimization_barrier(jnp.sum(weighted * attention, -1))
        d_attention = keep_scale * inverse[:, None] * (weighted - attention * (inverse * inverse * cross / feature_count)[:, None])
        grad_blocks = to_bf16_and_back(d_attention).reshape(block_count, BLK, H, DH)
        grads_gain.append(keep_scale * lax.optimization_barrier(jnp.sum(upstream * attention * inverse[:, None], 0)))
        fronts = jnp.einsum('bthd,bthe->bhde', jnp.where(head_select[:, :, None, None], query_blocks, 0.0), grad_blocks, precision=HIGH)
        bwd_segs, bwd_states = running_states(fronts, seg_values[:, 0], True)
        seen_bwd = seg_values == bwd_segs[:, None]

        def backward_block(pieces):
            query_one, key_one, value_one, grad_one, mask_one, seen_one, state_one, later_one, later_state = pieces
            scores = jnp.einsum('thd,shd->hts', query_one, key_one, precision=HIGH)
            weights = to_bf16_and_back(jnp.where(mask_one[None], scores, 0.0))
            grad_scores = jnp.einsum('thd,shd->hts', grad_one, value_one, precision=HIGH)
            grad_weights = to_bf16_and_back(jnp.where(mask_one[None], grad_scores, 0.0))
            fwd_round = to_bf16_and_back(state_one)
            bwd_round = to_bf16_and_back(later_state)
            query_part = jnp.einsum('hts,shd->thd', grad_weights, key_one, precision=HIGH)
            query_part = query_part + jnp.where(seen_one[:, None, None], jnp.einsum('the,hde->thd', grad_one, fwd_round, precision=HIGH), 0.0)
            key_part = jnp.einsum('hts,thd->shd', grad_weights, query_one, precision=HIGH)
            key_part = key_part + jnp.where(later_one[:, None, None], jnp.einsum('she,hde->shd', value_one, bwd_round, precision=HIGH), 0.0)
            value_part = jnp.einsum('hts,thd->shd', weights, grad_one, precision=HIGH)
            value_part = value_part + jnp.where(later_one[:, None, None], jnp.einsum('shd,hde->she', key_one, bwd_round, precision=HIGH), 0.0)
            return (query_part.astype(jnp.bfloat16), key_part.astype(jnp.bfloat16), value_part.astype(jnp.bfloat16))
        query_part, key_part, value_part = lax.map(backward_block, (query_blocks, key_blocks, value_blocks, grad_blocks, within, seen_fwd, fwd_states, seen_bwd, bwd_states))
        grads_query.append(query_part.reshape(TOKENS, feature_count))
        grads_key.append(key_part.reshape(TOKENS, feature_count))
        grads_value.append(value_part.reshape(TOKENS, feature_count))
    return (jnp.stack(grads_query), jnp.stack(grads_key), jnp.stack(grads_value), jnp.stack(grads_gain))
```

```python
import functools

import jax
import jax.numpy as jnp
from jax import lax
from jax.experimental import pallas as pl
from jax.experimental.pallas import tpu as pltpu
from jax.sharding import PartitionSpec as P

DH = 128
BLK = 256
EPSILON = 1e-06
KEEP_RATE = 0.75
F32 = jnp.float32
BF16 = jnp.bfloat16
MESH = pl.DeviceIdType.MESH


def dot(a, b, ca, cb):
    return lax.dot_general(a, b, (((ca,), (cb,)), ((), ())), preferred_element_type=F32)


def same(a, b):
    return jnp.where(a == b, 1.0, 0.0).astype(F32)


def kernel(
    nz, nf, layers, rows, heads,
    q_hbm, k_hbm, v_hbm, g_hbm, gain_ref, keep_ref, seg_ref,
    dq_ref, dk_ref, dv_ref, gg_ref,
    q_ref, k_ref, v_ref, g_ref, ld_sem,
    segrow, segcol, mask, maskt, mytile, ptile, tabz,
    tails, fronts, cq, qs, qmt, ks, vs, pt, o_ref, do_ref, kpart, vpart,
    dsum, dpart, tot, slots, ebuf, ein, xbuf, dev,
    stat, gtile, gptile, gsum, gslots,
    tile_s, tile_r, tab_s, tab_r,
    d_s, d_r, a_s, a_r, e_s, e_r, x_s, x_r,
    st_s, st_r, gt_s, gt_r, gz_s, gz_r,
):
    nb = rows // BLK
    cut = DH // nz
    features = heads * DH * nf
    s = lax.axis_index("seq")
    f = lax.axis_index("fsdp")
    z = s // 2
    c = s % 2
    partner = (2 * z + 1 - c, f)
    pending = []

    def zmod(x):
        return lax.rem(x + 2 * nz, nz)

    def zpeer(j):
        return (2 * zmod(z + j) + c, f)

    def fpeer(j):
        return (s, lax.rem(f + j, nf))

    def send(src, dst, ss, rs, to):
        copy = pltpu.make_async_remote_copy(
            src_ref=src, dst_ref=dst, send_sem=ss, recv_sem=rs, device_id=to, device_id_type=MESH
        )
        copy.start()
        pending.append(copy)

    def arrived(src, dst, ss, rs, to):
        pltpu.make_async_remote_copy(
            src_ref=src, dst_ref=dst, send_sem=ss, recv_sem=rs, device_id=to, device_id_type=MESH
        ).wait_recv()

    def flush():
        for copy in pending:
            copy.wait_send()
        pending.clear()

    def load(i, hbm, ref, l):
        return pltpu.make_async_copy(hbm.at[l], ref.at[l], ld_sem.at[i, l])

    for l in range(layers):
        load(0, k_hbm, k_ref, l).start()
        load(1, v_hbm, v_ref, l).start()
    for l in range(layers):
        load(2, q_hbm, q_ref, l).start()
    for l in range(layers):
        load(3, g_hbm, g_ref, l).start()

    barrier = pltpu.get_barrier_semaphore()
    pl.semaphore_signal(barrier, inc=1, device_id=partner, device_id_type=MESH)
    for j in range(1, nz):
        pl.semaphore_signal(barrier, inc=1, device_id=zpeer(j), device_id_type=MESH)
    for j in range(1, nf):
        pl.semaphore_signal(barrier, inc=1, device_id=fpeer(j), device_id_type=MESH)

    seg = seg_ref[...].astype(F32)
    for i in range(rows // 128):
        segrow[0:1, 128 * i : 128 * (i + 1)] = seg[i : i + 1, :]
        segcol[128 * i : 128 * (i + 1), :] = jnp.broadcast_to(seg[i : i + 1, :], (128, 128)).T
    first = [segcol[BLK * b : BLK * b + 1, :] for b in range(nb)]
    last = [segcol[BLK * b + BLK - 1 : BLK * b + BLK, :] for b in range(nb)]
    tile_row = lax.broadcasted_iota(jnp.int32, (8, 128), 0)
    mytile[...] = jnp.where(
        tile_row == 2 * c, first[0], jnp.where(tile_row == 2 * c + 1, last[nb - 1], 0.0)
    )

    def blk(b):
        return slice(BLK * b, BLK * (b + 1))

    def hd(h):
        return slice(DH * h, DH * (h + 1))

    def column_mask(b, value):
        return same(segcol[blk(b), :], value).astype(BF16)

    def hand_over(w, l):
        send(dsum.at[w, l, 1 - c], dpart.at[w, l], d_s.at[w, l], d_r.at[w, l], partner)

    def chip_total(w, l, own_weight, partner_weight):
        arrived(dsum.at[w, l, 1 - c], dpart.at[w, l], d_s.at[w, l], d_r.at[w, l], partner)
        total = own_weight * dsum[w, l, c] + partner_weight * dpart[w, l]
        tot[w, l] = total
        for j in range(1, nz):
            at = pl.multiple_of(zmod(z + j) * cut, cut)
            send(
                tot.at[w, l, pl.ds(at, cut)], slots.at[w, l, z],
                a_s.at[w, l, j - 1], a_r.at[w, l, j - 1], zpeer(j),
            )
        slots[w, l, z] = tot[w, l, pl.ds(pl.multiple_of(z * cut, cut), cut)]

    def owner(w, l):
        for j in range(1, nz):
            arrived(
                tot.at[w, l, pl.ds(0, cut)], slots.at[w, l, zmod(z - j)],
                a_s.at[w, l, j - 1], a_r.at[w, l, j - 1], zpeer(j),
            )
        if w == 0:
            edge = [tabz[i, 3:4, :] for i in range(nz)]
            order = list(range(nz))
        else:
            edge = [tabz[i, 0:1, :] for i in range(nz)]
            order = list(range(nz))[::-1]
        state = jnp.zeros((cut, DH), F32)
        for n, i in enumerate(order):
            if n == 1:
                state = slots[w, l, order[0]]
            elif n > 1:
                state = slots[w, l, order[n - 1]] + same(edge[order[n - 2]], edge[order[n - 1]]) * state
            ebuf[w, l, i] = state
        for j in range(1, nz):
            send(
                ebuf.at[w, l, zmod(z + j)],
                ein.at[w, l, pl.ds(pl.multiple_of(z * cut, cut), cut)],
                e_s.at[w, l, j - 1], e_r.at[w, l, j - 1], zpeer(j),
            )
        ein[w, l, pl.ds(pl.multiple_of(z * cut, cut), cut)] = ebuf[w, l, z]

    def entering(w, l, joined):
        for j in range(1, nz):
            at = pl.multiple_of(zmod(z - j) * cut, cut)
            arrived(
                ebuf.at[w, l, 0], ein.at[w, l, pl.ds(at, cut)],
                e_s.at[w, l, j - 1], e_r.at[w, l, j - 1], zpeer(j),
            )
        state = ein[w, l]
        second = c == 1 - w
        own_weight = jnp.where(second, joined, 1.0)
        partner_weight = jnp.where(second, 1.0, joined)
        zero = jnp.zeros((1, DH), F32)
        own_add = jnp.where(second, zero + 1.0, zero)
        partner_add = jnp.where(second, zero, zero + 1.0)
        xbuf[w, l] = partner_weight * state + partner_add * dsum[w, l, c]
        send(xbuf.at[w, l], dev.at[w, l, c], x_s.at[w, l], x_r.at[w, l], partner)
        dev[w, l, c] = own_weight * state + own_add * dpart[w, l]

    def entered(w, l):
        arrived(xbuf.at[w, l], dev.at[w, l, 1 - c], x_s.at[w, l], x_r.at[w, l], partner)

    tail_masks = [column_mask(b, last[b]) for b in range(nb)]
    for l in range(layers):
        load(0, k_hbm, k_ref, l).wait()
        load(1, v_hbm, v_ref, l).wait()
        for h in range(heads):
            total = None
            for b in range(nb):
                part = dot(k_ref[l, blk(b), hd(h)], v_ref[l, blk(b), hd(h)] * tail_masks[b], 0, 0)
                tails[l, h, b] = part
                part = part * same(last[b], last[nb - 1])
                total = part if total is None else total + part
            dsum[0, l, h] = total
        if l == 0:
            pl.semaphore_wait(barrier, 1 + (nz - 1) + (nf - 1))
            send(mytile, ptile, tile_s, tile_r, partner)
        hand_over(0, l)

    arrived(mytile, ptile, tile_s, tile_r, partner)
    chiptile = mytile[...] + ptile[...]
    tabz[z] = chiptile
    for j in range(1, nz):
        send(tabz.at[z], tabz.at[z], tab_s.at[j - 1], tab_r.at[j - 1], zpeer(j))
    first0, last0 = chiptile[0:1], chiptile[1:2]
    first1, last1 = chiptile[2:3], chiptile[3:4]
    is0 = c == 0
    end_own = jnp.where(is0, same(last0, last1), 1.0)
    end_partner = jnp.where(is0, 1.0, same(last0, last1))
    begin_own = jnp.where(is0, 1.0, same(first0, first1))
    begin_partner = jnp.where(is0, same(first0, first1), 1.0)
    for l in range(layers):
        chip_total(0, l, end_own, end_partner)

    at_t = lax.broadcasted_iota(jnp.int32, (BLK, BLK), 0)
    at_s = lax.broadcasted_iota(jnp.int32, (BLK, BLK), 1)
    for b in range(nb):
        wide = jnp.concatenate([segcol[blk(b), :]] * (BLK // 128), axis=1)
        equal = wide == segrow[0:1, blk(b)]
        mask[b] = jnp.where(jnp.logical_and(equal, at_t >= at_s), 1.0, 0.0).astype(BF16)
        maskt[b] = jnp.where(jnp.logical_and(equal, at_s >= at_t), 1.0, 0.0).astype(BF16)

    for l in range(layers):
        load(2, q_hbm, q_ref, l).wait()

    def inner(l, carry):
        for h in range(heads):
            for b in range(nb):
                scores = dot(q_ref[l, blk(b), hd(h)], k_ref[l, blk(b), hd(h)], 1, 1)
                weights = scores.astype(BF16) * mask[b]
                o_ref[l, blk(b), hd(h)] = dot(weights, v_ref[l, blk(b), hd(h)], 1, 0)
        return carry

    lax.fori_loop(0, layers, inner, 0)

    for j in range(1, nz):
        arrived(tabz.at[z], tabz.at[zmod(z - j)], tab_s.at[j - 1], tab_r.at[j - 1], zpeer(j))
    for l in range(layers):
        owner(0, l)

    before_chip = tabz[zmod(z - 1), 3:4, :]
    after_chip = tabz[zmod(z + 1), 0:1, :]
    before = jnp.where(is0, before_chip, last0)
    after = jnp.where(is0, first1, after_chip)
    prior = [before] + last[: nb - 1]
    later = first[1:] + [after]

    def prepare(l, carry):
        for b in range(nb):
            seen_f = column_mask(b, prior[b])
            seen_b = column_mask(b, later[b])
            head = column_mask(b, first[b])
            for h in range(heads):
                q = q_ref[l, blk(b), hd(h)]
                k = k_ref[l, blk(b), hd(h)]
                qs[l, blk(b), hd(h)] = q * seen_f
                qmt[l, hd(h), blk(b)] = (q * head).T
                ks[l, blk(b), hd(h)] = k * seen_b
                vs[l, blk(b), hd(h)] = v_ref[l, blk(b), hd(h)] * seen_b
                pt[l, h, b] = dot(k, q, 1, 1).astype(BF16) * maskt[b]
        return carry

    lax.fori_loop(0, layers, prepare, 0)

    for l in range(layers):
        load(3, g_hbm, g_ref, l).wait()
    joined = same(before_chip, last0)
    for l in range(layers):
        entering(0, l, joined)

    ones = jnp.ones((8, DH), BF16)

    def sums(x):
        high = x.astype(BF16)
        low = (x - high.astype(F32)).astype(BF16)
        total = dot(ones, high, 1, 1) + dot(ones, low, 1, 1)
        tile = jnp.zeros((8, 128), F32)
        for i in range(rows // 128):
            tile = jnp.where(tile_row == i, total[:, 128 * i : 128 * (i + 1)], tile)
        return tile

    for l in range(layers):
        entered(0, l)
        for h in range(heads):
            state = dev[0, l, h]
            for b in range(nb):
                if b:
                    state = tails[l, h, b - 1] + same(prior[b - 1], prior[b]) * state
                cq[l, h, b] = state.astype(BF16)
        squares, crosses = [], []
        for b in range(nb):
            square, cross = None, None
            for h in range(heads):
                o = o_ref[l, blk(b), hd(h)] + dot(qs[l, blk(b), hd(h)], cq[l, h, b], 1, 0)
                o_ref[l, blk(b), hd(h)] = o
                a = g_ref[l, blk(b), hd(h)].astype(F32) * gain_ref[l : l + 1, hd(h)]
                square = o * o if square is None else square + o * o
                cross = a * o if cross is None else cross + a * o
            squares.append(square)
            crosses.append(cross)
        stat[l, f, 0:8, :] = sums(jnp.concatenate(squares, axis=0))
        stat[l, f, 8:16, :] = sums(jnp.concatenate(crosses, axis=0))
        for j in range(1, nf):
            send(stat.at[l, f], stat.at[l, f], st_s.at[l, j - 1], st_r.at[l, j - 1], fpeer(j))

    for l in range(layers):
        for j in range(1, nf):
            arrived(
                stat.at[l, f], stat.at[l, lax.rem(f + nf - j, nf)],
                st_s.at[l, j - 1], st_r.at[l, j - 1], fpeer(j),
            )
        both = stat[l, 0]
        for i in range(1, nf):
            both = both + stat[l, i]
        r = lax.rsqrt(both[0:8] / features + EPSILON)
        keep = keep_ref[l].astype(F32) / KEEP_RATE
        scale_a = keep * r
        scale_o = scale_a * (r * r) * (both[8:16] / features)
        turned = jnp.concatenate([scale_a, scale_o, jnp.zeros((112, 128), F32)], axis=0).T
        gains = [jnp.zeros((1, DH), F32) for h in range(heads)]
        totals = [None] * heads
        for b in range(nb):
            per = BLK // 128
            col_a = jnp.concatenate(
                [jnp.broadcast_to(turned[:, per * b + i : per * b + i + 1], (128, 128)) for i in range(per)], axis=0
            )
            col_o = jnp.concatenate(
                [jnp.broadcast_to(turned[:, 8 + per * b + i : 9 + per * b + i], (128, 128)) for i in range(per)], axis=0
            )
            for h in range(heads):
                o = o_ref[l, blk(b), hd(h)]
                up = g_ref[l, blk(b), hd(h)].astype(F32) * col_a
                gains[h] = gains[h] + jnp.sum(up * o, axis=0, keepdims=True)
                grad = (up * gain_ref[l : l + 1, hd(h)] - o * col_o).astype(BF16)
                do_ref[l, blk(b), hd(h)] = grad
                part = dot(qmt[l, hd(h), blk(b)], grad, 1, 0)
                fronts[l, h, b] = part
                part = part * same(first[b], first[0])
                totals[h] = part if totals[h] is None else totals[h] + part
        for h in range(heads):
            dsum[1, l, h] = totals[h]
            gtile[heads * l + h : heads * l + h + 1, :] = gains[h]
        hand_over(1, l)
    for i in range(heads * layers, 8):
        gtile[i : i + 1, :] = jnp.zeros((1, DH), F32)
    send(gtile, gptile, gt_s, gt_r, partner)
    for l in range(layers):
        chip_total(1, l, begin_own, begin_partner)

    def outer(l, carry):
        for h in range(heads):
            for b in range(nb):
                grad = do_ref[l, blk(b), hd(h)]
                v = v_ref[l, blk(b), hd(h)]
                vpart[l, blk(b), hd(h)] = dot(pt[l, h, b], grad, 1, 0)
                gst = dot(v, grad, 1, 1).astype(BF16) * maskt[b]
                kpart[l, blk(b), hd(h)] = dot(gst, q_ref[l, blk(b), hd(h)], 1, 0)
        return carry

    lax.fori_loop(0, layers, outer, 0)
    arrived(gtile, gptile, gt_s, gt_r, partner)
    gslots[z] = gtile[...] + gptile[...]
    for j in range(1, nz):
        send(gslots.at[z], gslots.at[z], gz_s.at[j - 1], gz_r.at[j - 1], zpeer(j))
    for l in range(layers):
        owner(1, l)

    def outer_q(l, carry):
        for h in range(heads):
            for b in range(nb):
                grad = do_ref[l, blk(b), hd(h)]
                gs = dot(grad, v_ref[l, blk(b), hd(h)], 1, 1).astype(BF16) * mask[b]
                seen_f = column_mask(b, prior[b])
                dq_ref[l, blk(b), hd(h)] = (
                    dot(gs, k_ref[l, blk(b), hd(h)], 1, 0) + dot(grad * seen_f, cq[l, h, b], 1, 1)
                ).astype(BF16)
        return carry

    lax.fori_loop(0, layers, outer_q, 0)
    for j in range(1, nz):
        arrived(gslots.at[z], gslots.at[zmod(z - j)], gz_s.at[j - 1], gz_r.at[j - 1], zpeer(j))
    gtotal = gslots[0]
    for i in range(1, nz):
        gtotal = gtotal + gslots[i]
    for l in range(layers):
        for h in range(heads):
            gg_ref[l : l + 1, hd(h)] = gtotal[heads * l + h : heads * l + h + 1, :]

    joined = same(after_chip, first1)
    for l in range(layers):
        entering(1, l, joined)
    flush()

    for l in range(layers):
        entered(1, l)
        for h in range(heads):
            state = dev[1, l, h]
            for b in range(nb)[::-1]:
                if b < nb - 1:
                    state = fronts[l, h, b + 1] + same(later[b + 1], later[b]) * state
                rq = state.astype(BF16)
                dk_ref[l, blk(b), hd(h)] = (
                    kpart[l, blk(b), hd(h)] + dot(vs[l, blk(b), hd(h)], rq, 1, 1)
                ).astype(BF16)
                dv_ref[l, blk(b), hd(h)] = (
                    vpart[l, blk(b), hd(h)] + dot(ks[l, blk(b), hd(h)], rq, 1, 0)
                ).astype(BF16)


def local(queries, keys, values, out_grad, gain, keep_mask, segments):
    layers, rows, channels = queries.shape
    heads = channels // DH
    nz = lax.axis_size("seq") // 2
    nf = lax.axis_size("fsdp")
    nb = rows // BLK
    cut = DH // nz
    whole = (layers, rows, channels)
    vmem = pltpu.VMEM
    dma = pltpu.SemaphoreType.DMA
    hbm = pl.BlockSpec(memory_space=pl.ANY)
    near = pl.BlockSpec(memory_space=pltpu.VMEM)
    scratch = [
        vmem(whole, BF16), vmem(whole, BF16), vmem(whole, BF16), vmem(whole, BF16), dma((4, layers)),
        vmem((1, rows), F32), vmem((rows, 128), F32), vmem((nb, BLK, BLK), BF16), vmem((nb, BLK, BLK), BF16),
        vmem((8, 128), F32), vmem((8, 128), F32), vmem((nz, 8, 128), F32),
        vmem((layers, heads, nb, DH, DH), F32), vmem((layers, heads, nb, DH, DH), F32),
        vmem((layers, heads, nb, DH, DH), BF16),
        vmem(whole, BF16), vmem((layers, channels, rows), BF16), vmem(whole, BF16), vmem(whole, BF16),
        vmem((layers, heads, nb, BLK, BLK), BF16),
        vmem(whole, F32), vmem(whole, BF16), vmem(whole, F32), vmem(whole, F32),
        vmem((2, layers, heads, DH, DH), F32), vmem((2, layers, DH, DH), F32), vmem((2, layers, DH, DH), F32),
        vmem((2, layers, nz, cut, DH), F32), vmem((2, layers, nz, cut, DH), F32),
        vmem((2, layers, DH, DH), F32), vmem((2, layers, DH, DH), F32), vmem((2, layers, heads, DH, DH), F32),
        vmem((layers, nf, 16, 128), F32),
        vmem((8, 128), F32), vmem((8, 128), F32), vmem((8, 128), F32), vmem((nz, 8, 128), F32),
        dma, dma, dma((nz - 1,)), dma((nz - 1,)),
        dma((2, layers)), dma((2, layers)),
        dma((2, layers, nz - 1)), dma((2, layers, nz - 1)),
        dma((2, layers, nz - 1)), dma((2, layers, nz - 1)),
        dma((2, layers)), dma((2, layers)),
        dma((layers, nf - 1)), dma((layers, nf - 1)),
        dma, dma, dma((nz - 1,)), dma((nz - 1,)),
    ]
    return pl.pallas_call(
        functools.partial(kernel, nz, nf, layers, rows, heads),
        out_shape=(
            jax.ShapeDtypeStruct(whole, BF16),
            jax.ShapeDtypeStruct(whole, BF16),
            jax.ShapeDtypeStruct(whole, BF16),
            jax.ShapeDtypeStruct((layers, channels), F32),
        ),
        in_specs=[hbm, hbm, hbm, hbm, near, pl.BlockSpec(memory_space=pltpu.SMEM), near],
        out_specs=(near, near, near, near),
        scratch_shapes=scratch,
        compiler_params=pltpu.CompilerParams(
            collective_id=0, has_side_effects=True, vmem_limit_bytes=56 * 2**20
        ),
        name="backward",
    )(queries, keys, values, out_grad, gain, keep_mask, segments.reshape(rows // 128, 128))


def solution(mesh):
    wide = P(None, "seq", "fsdp")
    in_specs = (wide, wide, wide, wide, P(None, "fsdp"), P(), P("seq"))
    out_specs = (wide, wide, wide, P(None, "fsdp"))
    return jax.shard_map(local, mesh=mesh, in_specs=in_specs, out_specs=out_specs, check_vma=False)
```

```python
import functools

import jax
import jax.numpy as jnp
from jax import lax
from jax.experimental import pallas as pl
from jax.experimental.pallas import tpu as pltpu
from jax.sharding import PartitionSpec as P

DH = 128
BLK = 256
EPSILON = 1e-06
KEEP_RATE = 0.75
F32 = jnp.float32
BF16 = jnp.bfloat16
MESH = pl.DeviceIdType.MESH


def dot(a, b, ca, cb):
    return lax.dot_general(a, b, (((ca,), (cb,)), ((), ())), preferred_element_type=F32)


def same(a, b):
    return jnp.where(a == b, 1.0, 0.0).astype(F32)


def kernel(
    nz, nf, layers, rows, heads,
    q_hbm, k_hbm, v_hbm, g_hbm, gain_hbm, keep_ref, seg_hbm,
    dq_out, kpart_out, vpart_out, ks_out, vs_out, rq_out, gg_out,
    q_ref, k_ref, v_ref, g_ref, ld_sem, qg_sem, gain_ref, seg_ref, small_sem, out_sem,
    dq_ref, rq_ref, gg_ref,
    segrow, segcol, mask, maskt, mytile, ptile, tabz,
    tails, fronts, cq, qs, qmt, ks, vs, pt, o_ref, do_ref, kpart, vpart,
    dsum, dpart, tot, slots, ebuf, ein, xbuf, dev,
    stat, gtile, gptile, gslots,
    tile_s, tile_r, tab_s, tab_r,
    d_s, d_r, a_s, a_r, e_s, e_r, x_s, x_r,
    st_s, st_r, gt_s, gt_r, gz_s, gz_r,
):
    nb = rows // BLK
    cut = DH // nz
    steps = sorted(range(1, nz), key=lambda j: -min(j, nz - j))
    features = heads * DH * nf
    s = lax.axis_index("seq")
    f = lax.axis_index("fsdp")
    z = s // 2
    c = s % 2
    partner = (2 * z + 1 - c, f)

    def zmod(x):
        return lax.rem(x + 2 * nz, nz)

    def zpeer(j):
        return (2 * zmod(z + j) + c, f)

    def fpeer(j):
        return (s, lax.rem(f + j, nf))

    def remote(src, dst, ss, rs, to):
        return pltpu.make_async_remote_copy(
            src_ref=src, dst_ref=dst, send_sem=ss, recv_sem=rs, device_id=to, device_id_type=MESH
        )

    def sent(part, sem):
        remote(part, part, sem, sem, partner).wait_send()

    def arrived(part, sem):
        remote(part, part, sem, sem, partner).wait_recv()

    def load(i, hbm, ref, l):
        return pltpu.make_async_copy(hbm.at[l], ref.at[l], ld_sem.at[i, l])

    small = (
        pltpu.make_async_copy(seg_hbm, seg_ref, small_sem.at[0]),
        pltpu.make_async_copy(gain_hbm, gain_ref, small_sem.at[1]),
        pltpu.make_async_copy(gg_ref, gg_out, small_sem.at[2]),
    )
    small[0].start()
    load(0, k_hbm, k_ref, 0).start()
    load(1, v_hbm, v_ref, 0).start()
    whole_loads = (
        pltpu.make_async_copy(q_hbm, q_ref, qg_sem.at[0]),
        pltpu.make_async_copy(g_hbm, g_ref, qg_sem.at[1]),
    )

    store_dq, store_k, store_v, store_ks, store_vs, store_rq = (
        pltpu.make_async_copy(ref, out, out_sem.at[i])
        for i, (ref, out) in enumerate((
            (dq_ref, dq_out), (kpart, kpart_out), (vpart, vpart_out),
            (ks, ks_out), (vs, vs_out), (rq_ref, rq_out),
        ))
    )

    barrier = pltpu.get_barrier_semaphore()
    pl.semaphore_signal(barrier, inc=1, device_id=partner, device_id_type=MESH)
    for j in range(1, nz):
        pl.semaphore_signal(barrier, inc=1, device_id=zpeer(j), device_id_type=MESH)
    for j in range(1, nf):
        pl.semaphore_signal(barrier, inc=1, device_id=fpeer(j), device_id_type=MESH)

    small[0].wait()
    for l in range(1, layers):
        load(0, k_hbm, k_ref, l).start()
        load(1, v_hbm, v_ref, l).start()
    seg = seg_ref[...].astype(F32)
    for i in range(rows // 128):
        segrow[0:1, 128 * i : 128 * (i + 1)] = seg[i : i + 1, :]
        segcol[128 * i : 128 * (i + 1), :] = jnp.broadcast_to(seg[i : i + 1, :], (128, 128)).T
    first = [segcol[BLK * b : BLK * b + 1, :] for b in range(nb)]
    last = [segcol[BLK * b + BLK - 1 : BLK * b + BLK, :] for b in range(nb)]
    tile_row = lax.broadcasted_iota(jnp.int32, (8, 128), 0)
    mytile[...] = jnp.where(
        tile_row == 2 * c, first[0], jnp.where(tile_row == 2 * c + 1, last[nb - 1], 0.0)
    )

    def blk(b):
        return slice(BLK * b, BLK * (b + 1))

    def hd(h):
        return slice(DH * h, DH * (h + 1))

    def column_mask(b, value):
        return same(segcol[blk(b), :], value).astype(BF16)

    def hand_over(w, l):
        remote(dsum.at[w, l, 1 - c], dpart.at[w, l], d_s.at[w], d_r.at[w, l], partner).start()

    def chip_total(w, l, own_weight, partner_weight):
        arrived(dpart.at[w, l], d_r.at[w, l])
        total = own_weight * dsum[w, l, c] + partner_weight * dpart[w, l]
        tot[w, l] = total
        for j in steps:
            at = pl.multiple_of(zmod(z + j) * cut, cut)
            remote(
                tot.at[w, l, pl.ds(at, cut)], slots.at[w, l, z], a_s.at[w], a_r.at[w, l], zpeer(j)
            ).start()
        slots[w, l, z] = tot[w, l, pl.ds(pl.multiple_of(z * cut, cut), cut)]

    def owner(w, l):
        arrived(slots.at[w, l, 0 : nz - 1], a_r.at[w, l])
        if w == 0:
            edge = [tabz[i, 3:4, :] for i in range(nz)]
            order = list(range(nz))
        else:
            edge = [tabz[i, 0:1, :] for i in range(nz)]
            order = list(range(nz))[::-1]
        state = jnp.zeros((cut, DH), F32)
        for n, i in enumerate(order):
            if n == 1:
                state = slots[w, l, order[0]]
            elif n > 1:
                state = slots[w, l, order[n - 1]] + same(edge[order[n - 2]], edge[order[n - 1]]) * state
            ebuf[w, l, i] = state
        for j in steps:
            remote(
                ebuf.at[w, l, zmod(z + j)],
                ein.at[w, l, pl.ds(pl.multiple_of(z * cut, cut), cut)],
                e_s.at[w], e_r.at[w, l], zpeer(j),
            ).start()
        ein[w, l, pl.ds(pl.multiple_of(z * cut, cut), cut)] = ebuf[w, l, z]

    def entering(w, l, joined):
        arrived(ein.at[w, l, 0 : DH - cut], e_r.at[w, l])
        state = ein[w, l]
        second = c == 1 - w
        own_weight = jnp.where(second, joined, 1.0)
        partner_weight = jnp.where(second, 1.0, joined)
        zero = jnp.zeros((1, DH), F32)
        own_add = jnp.where(second, zero + 1.0, zero)
        partner_add = jnp.where(second, zero, zero + 1.0)
        xbuf[w, l] = partner_weight * state + partner_add * dsum[w, l, c]
        remote(xbuf.at[w, l], dev.at[w, l, c], x_s.at[w], x_r.at[w, l], partner).start()
        dev[w, l, c] = own_weight * state + own_add * dpart[w, l]

    def entered(w, l):
        arrived(dev.at[w, l, 1 - c], x_r.at[w, l])

    def sent_state(w):
        sent(dsum.at[w, :, 0], d_s.at[w])
        sent(tot.at[w, :, 0 : DH - cut], a_s.at[w])
        sent(ebuf.at[w, :, 0 : nz - 1], e_s.at[w])
        sent(xbuf.at[w], x_s.at[w])

    tail_masks = [column_mask(b, last[b]) for b in range(nb)]
    for l in range(layers):
        load(0, k_hbm, k_ref, l).wait()
        load(1, v_hbm, v_ref, l).wait()
        for h in range(heads):
            total = None
            for b in range(nb):
                part = dot(k_ref[l, blk(b), hd(h)], v_ref[l, blk(b), hd(h)] * tail_masks[b], 0, 0)
                tails[l, h, b] = part
                part = part * same(last[b], last[nb - 1])
                total = part if total is None else total + part
            dsum[0, l, h] = total
    pl.semaphore_wait(barrier, 1 + (nz - 1) + (nf - 1))
    remote(mytile, ptile, tile_s, tile_r, partner).start()
    for l in range(layers):
        hand_over(0, l)
    for copy in whole_loads:
        copy.start()
    small[1].start()

    arrived(ptile, tile_r)
    chiptile = mytile[...] + ptile[...]
    tabz[z] = chiptile
    for j in steps:
        remote(tabz.at[z], tabz.at[z], tab_s, tab_r, zpeer(j)).start()
    first0, last0 = chiptile[0:1], chiptile[1:2]
    first1, last1 = chiptile[2:3], chiptile[3:4]
    is0 = c == 0
    end_own = jnp.where(is0, same(last0, last1), 1.0)
    end_partner = jnp.where(is0, 1.0, same(last0, last1))
    begin_own = jnp.where(is0, 1.0, same(first0, first1))
    begin_partner = jnp.where(is0, same(first0, first1), 1.0)
    for l in range(layers):
        chip_total(0, l, end_own, end_partner)

    at_t = lax.broadcasted_iota(jnp.int32, (BLK, BLK), 0)
    at_s = lax.broadcasted_iota(jnp.int32, (BLK, BLK), 1)
    for b in range(nb):
        wide = jnp.concatenate([segcol[blk(b), :]] * (BLK // 128), axis=1)
        equal = wide == segrow[0:1, blk(b)]
        mask[b] = jnp.where(jnp.logical_and(equal, at_t >= at_s), 1.0, 0.0).astype(BF16)
        maskt[b] = jnp.where(jnp.logical_and(equal, at_s >= at_t), 1.0, 0.0).astype(BF16)

    whole_loads[0].wait()

    def inner(l, carry):
        for h in range(heads):
            for b in range(nb):
                scores = dot(q_ref[l, blk(b), hd(h)], k_ref[l, blk(b), hd(h)], 1, 1)
                weights = scores.astype(BF16) * mask[b]
                o_ref[l, blk(b), hd(h)] = dot(weights, v_ref[l, blk(b), hd(h)], 1, 0)
        return carry

    lax.fori_loop(0, layers, inner, 0)

    arrived(tabz.at[0 : nz - 1], tab_r)
    for l in range(layers):
        owner(0, l)

    before_chip = tabz[zmod(z - 1), 3:4, :]
    after_chip = tabz[zmod(z + 1), 0:1, :]
    before = jnp.where(is0, before_chip, last0)
    after = jnp.where(is0, first1, after_chip)
    prior = [before] + last[: nb - 1]
    later = first[1:] + [after]

    def prepare(l, carry):
        for b in range(nb):
            seen_f = column_mask(b, prior[b])
            seen_b = column_mask(b, later[b])
            head = column_mask(b, first[b])
            for h in range(heads):
                q = q_ref[l, blk(b), hd(h)]
                k = k_ref[l, blk(b), hd(h)]
                qs[l, blk(b), hd(h)] = q * seen_f
                qmt[l, hd(h), blk(b)] = (q * head).T
                ks[l, blk(b), hd(h)] = k * seen_b
                vs[l, blk(b), hd(h)] = v_ref[l, blk(b), hd(h)] * seen_b
                pt[l, h, b] = dot(k, q, 1, 1).astype(BF16) * maskt[b]
        return carry

    lax.fori_loop(0, layers, prepare, 0)

    whole_loads[1].wait()
    store_ks.start()
    store_vs.start()
    small[1].wait()
    joined = same(before_chip, last0)

    ones = jnp.ones((8, 2 * DH), BF16)

    def split(x):
        high = x.astype(BF16)
        return jnp.concatenate([high, (x - high.astype(F32)).astype(BF16)], axis=1)

    def carried(l):
        entered(0, l)
        for h in range(heads):
            state = dev[0, l, h]
            for b in range(nb):
                if b:
                    state = tails[l, h, b - 1] + same(prior[b - 1], prior[b]) * state
                cq[l, h, b] = state.astype(BF16)
        tiles = [jnp.zeros((8, 128), F32), jnp.zeros((8, 128), F32)]
        for b in range(nb):
            square, cross = None, None
            for h in range(heads):
                o = o_ref[l, blk(b), hd(h)] + dot(qs[l, blk(b), hd(h)], cq[l, h, b], 1, 0)
                o_ref[l, blk(b), hd(h)] = o
                a = g_ref[l, blk(b), hd(h)].astype(F32) * gain_ref[l : l + 1, hd(h)]
                square = o * o if square is None else square + o * o
                cross = a * o if cross is None else cross + a * o
            for n, x in enumerate((square, cross)):
                total = dot(ones, split(x), 1, 1)
                for i in range(BLK // 128):
                    tiles[n] = jnp.where(
                        tile_row == b * (BLK // 128) + i, total[:, 128 * i : 128 * (i + 1)], tiles[n]
                    )
        stat[l, f, 0:8, :] = tiles[0]
        stat[l, f, 8:16, :] = tiles[1]
        for j in range(1, nf):
            remote(stat.at[l, f], stat.at[l, f], st_s, st_r.at[l], fpeer(j)).start()

    for l in range(layers):
        entering(0, l, joined)
        if l > 0:
            carried(l - 1)
    carried(layers - 1)

    for l in range(layers):
        arrived(stat.at[l, 0 : nf - 1], st_r.at[l])
        both = stat[l, 0]
        for i in range(1, nf):
            both = both + stat[l, i]
        r = lax.rsqrt(both[0:8] / features + EPSILON)
        keep = keep_ref[l].astype(F32) / KEEP_RATE
        scale_a = keep * r
        scale_o = scale_a * (r * r) * (both[8:16] / features)
        turned = jnp.concatenate([scale_a, scale_o, jnp.zeros((112, 128), F32)], axis=0).T
        gains = [jnp.zeros((1, DH), F32) for h in range(heads)]
        totals = [None] * heads
        for b in range(nb):
            per = BLK // 128
            col_a = jnp.concatenate(
                [jnp.broadcast_to(turned[:, per * b + i : per * b + i + 1], (128, 128)) for i in range(per)], axis=0
            )
            col_o = jnp.concatenate(
                [jnp.broadcast_to(turned[:, 8 + per * b + i : 9 + per * b + i], (128, 128)) for i in range(per)], axis=0
            )
            for h in range(heads):
                o = o_ref[l, blk(b), hd(h)]
                up = g_ref[l, blk(b), hd(h)].astype(F32) * col_a
                gains[h] = gains[h] + jnp.sum(up * o, axis=0, keepdims=True)
                grad = (up * gain_ref[l : l + 1, hd(h)] - o * col_o).astype(BF16)
                do_ref[l, blk(b), hd(h)] = grad
                part = dot(qmt[l, hd(h), blk(b)], grad, 1, 0)
                fronts[l, h, b] = part
                part = part * same(first[b], first[0])
                totals[h] = part if totals[h] is None else totals[h] + part
        for h in range(heads):
            dsum[1, l, h] = totals[h]
            gtile[heads * l + h : heads * l + h + 1, :] = gains[h]
        hand_over(1, l)
        if l > 0:
            chip_total(1, l - 1, begin_own, begin_partner)
    for i in range(heads * layers, 8):
        gtile[i : i + 1, :] = jnp.zeros((1, DH), F32)
    remote(gtile, gptile, gt_s, gt_r, partner).start()
    chip_total(1, layers - 1, begin_own, begin_partner)

    def outer_head(l, h):
        for b in range(nb):
            grad = do_ref[l, blk(b), hd(h)]
            v = v_ref[l, blk(b), hd(h)]
            vpart[l, blk(b), hd(h)] = dot(pt[l, h, b], grad, 1, 0)
            gst = dot(v, grad, 1, 1).astype(BF16) * maskt[b]
            kpart[l, blk(b), hd(h)] = dot(gst, q_ref[l, blk(b), hd(h)], 1, 0)

    def outer(l, carry):
        for h in range(heads):
            outer_head(l, h)
        return carry

    lax.fori_loop(0, layers - 1, outer, 0)
    for h in range(heads - 1):
        outer_head(layers - 1, h)
    arrived(gptile, gt_r)
    gslots[z] = gtile[...] + gptile[...]
    for j in steps:
        remote(gslots.at[z], gslots.at[z], gz_s, gz_r, zpeer(j)).start()
    for l in range(layers - 1):
        owner(1, l)
    outer_head(layers - 1, heads - 1)
    owner(1, layers - 1)
    store_k.start()
    store_v.start()

    def outer_q(l, carry):
        for h in range(heads):
            for b in range(nb):
                grad = do_ref[l, blk(b), hd(h)]
                gs = dot(grad, v_ref[l, blk(b), hd(h)], 1, 1).astype(BF16) * mask[b]
                seen_f = column_mask(b, prior[b])
                dq_ref[l, blk(b), hd(h)] = (
                    dot(gs, k_ref[l, blk(b), hd(h)], 1, 0) + dot(grad * seen_f, cq[l, h, b], 1, 1)
                ).astype(BF16)
        return carry

    lax.fori_loop(0, layers, outer_q, 0)
    store_dq.start()
    sent(mytile, tile_s)
    sent(tabz.at[0 : nz - 1], tab_s)
    sent_state(0)
    sent(stat.at[:, 0 : nf - 1], st_s)
    sent(gtile, gt_s)

    joined = same(after_chip, first1)
    for l in range(layers):
        entering(1, l, joined)

    arrived(gslots.at[0 : nz - 1], gz_r)
    gtotal = gslots[0]
    for i in range(1, nz):
        gtotal = gtotal + gslots[i]
    for l in range(layers):
        for h in range(heads):
            gg_ref[l : l + 1, hd(h)] = gtotal[heads * l + h : heads * l + h + 1, :]
    small[2].start()
    sent(gslots.at[0 : nz - 1], gz_s)

    for l in range(layers):
        entered(1, l)
        for h in range(heads):
            state = dev[1, l, h]
            for b in range(nb)[::-1]:
                if b < nb - 1:
                    state = fronts[l, h, b + 1] + same(later[b + 1], later[b]) * state
                rq_ref[l, h, b] = state.astype(BF16)
    store_rq.start()
    sent_state(1)
    for copy in (store_ks, store_vs, store_k, store_v, store_dq, small[2], store_rq):
        copy.wait()


def finish(
    layers, rows, heads,
    dq_ref, kpart, vpart, ks, vs, rq, gg_ref,
    dq_hbm, dk_hbm, dv_hbm, gg_hbm,
    dk_ref, dv_ref, sem, gg_sem,
):
    nb = rows // BLK
    gg_copy = pltpu.make_async_copy(gg_ref, gg_hbm, gg_sem)
    gg_copy.start()

    def copy(i, ref, hbm, l):
        return pltpu.make_async_copy(ref.at[l], hbm.at[l], sem.at[i, l])

    for l in range(layers):
        copy(0, dq_ref, dq_hbm, l).start()
    for l in range(layers):
        for h in range(heads):
            for b in range(nb):
                at = (l, slice(BLK * b, BLK * (b + 1)), slice(DH * h, DH * (h + 1)))
                dk_ref[at] = (kpart[at] + dot(vs[at], rq[l, h, b], 1, 1)).astype(BF16)
                dv_ref[at] = (vpart[at] + dot(ks[at], rq[l, h, b], 1, 0)).astype(BF16)
        copy(1, dk_ref, dk_hbm, l).start()
        copy(2, dv_ref, dv_hbm, l).start()
    gg_copy.wait()
    for l in range(layers):
        copy(0, dq_ref, dq_hbm, l).wait()
        copy(1, dk_ref, dk_hbm, l).wait()
        copy(2, dv_ref, dv_hbm, l).wait()


def local(queries, keys, values, out_grad, gain, keep_mask, segments):
    layers, rows, channels = queries.shape
    heads = channels // DH
    nz = lax.axis_size("seq") // 2
    nf = lax.axis_size("fsdp")
    nb = rows // BLK
    cut = DH // nz
    whole = (layers, rows, channels)
    vmem = pltpu.VMEM
    dma = pltpu.SemaphoreType.DMA
    hbm = pl.BlockSpec(memory_space=pl.ANY)

    def far(x):
        return pltpu.with_memory_space_constraint(x, pltpu.HBM)

    near = pl.BlockSpec(memory_space=pltpu.VMEM)
    scratch = [
        vmem(whole, BF16), vmem(whole, BF16), vmem(whole, BF16), vmem(whole, BF16), dma((2, layers)), dma((2,)),
        vmem((layers, channels), F32), vmem((rows // 128, 128), jnp.int32), dma((3,)), dma((6,)),
        vmem(whole, BF16), vmem((layers, heads, nb, DH, DH), BF16), vmem((layers, channels), F32),
        vmem((1, rows), F32), vmem((rows, 128), F32), vmem((nb, BLK, BLK), BF16), vmem((nb, BLK, BLK), BF16),
        vmem((8, 128), F32), vmem((8, 128), F32), vmem((nz, 8, 128), F32),
        vmem((layers, heads, nb, DH, DH), F32), vmem((layers, heads, nb, DH, DH), F32),
        vmem((layers, heads, nb, DH, DH), BF16),
        vmem(whole, BF16), vmem((layers, channels, rows), BF16), vmem(whole, BF16), vmem(whole, BF16),
        vmem((layers, heads, nb, BLK, BLK), BF16),
        vmem(whole, F32), vmem(whole, BF16), vmem(whole, F32), vmem(whole, F32),
        vmem((2, layers, heads, DH, DH), F32), vmem((2, layers, DH, DH), F32), vmem((2, layers, DH, DH), F32),
        vmem((2, layers, nz, cut, DH), F32), vmem((2, layers, nz, cut, DH), F32),
        vmem((2, layers, DH, DH), F32), vmem((2, layers, DH, DH), F32), vmem((2, layers, heads, DH, DH), F32),
        vmem((layers, nf, 16, 128), F32),
        vmem((8, 128), F32), vmem((8, 128), F32), vmem((nz, 8, 128), F32),
        dma, dma, dma, dma,
        dma((2,)), dma((2, layers)),
        dma((2,)), dma((2, layers)),
        dma((2,)), dma((2, layers)),
        dma((2,)), dma((2, layers)),
        dma, dma((layers,)),
        dma, dma, dma, dma,
    ]
    results = pl.pallas_call(
        functools.partial(kernel, nz, nf, layers, rows, heads),
        out_shape=(
            vmem(whole, BF16),
            vmem(whole, F32),
            vmem(whole, F32),
            vmem(whole, BF16),
            vmem(whole, BF16),
            vmem((layers, heads, nb, DH, DH), BF16),
            vmem((layers, channels), F32),
        ),
        in_specs=[hbm, hbm, hbm, hbm, hbm, pl.BlockSpec(memory_space=pltpu.SMEM), hbm],
        out_specs=(hbm,) * 7,
        scratch_shapes=scratch,
        compiler_params=pltpu.CompilerParams(
            collective_id=0, has_side_effects=True, vmem_limit_bytes=44 * 2**20
        ),
        name="backward",
    )(
        far(queries), far(keys), far(values), far(out_grad), far(gain), keep_mask,
        far(segments.reshape(rows // 128, 128)),
    )
    return pl.pallas_call(
        functools.partial(finish, layers, rows, heads),
        out_shape=(
            jax.ShapeDtypeStruct(whole, BF16),
            jax.ShapeDtypeStruct(whole, BF16),
            jax.ShapeDtypeStruct(whole, BF16),
            jax.ShapeDtypeStruct((layers, channels), F32),
        ),
        in_specs=[near] * 7,
        out_specs=(hbm,) * 4,
        scratch_shapes=[vmem(whole, BF16), vmem(whole, BF16), dma((3, layers)), dma],
        compiler_params=pltpu.CompilerParams(vmem_limit_bytes=8 * 2**20),
        name="finish",
    )(*[pltpu.with_memory_space_constraint(result, pltpu.VMEM) for result in results])


def solution(mesh):
    wide = P(None, "seq", "fsdp")
    in_specs = (wide, wide, wide, wide, P(None, "fsdp"), P(), P("seq"))
    out_specs = (wide, wide, wide, P(None, "fsdp"))
    return jax.shard_map(local, mesh=mesh, in_specs=in_specs, out_specs=out_specs, check_vma=False)
```

```python
import functools
import math

import jax
import jax.numpy as jnp
from jax import lax
from jax.experimental import pallas as pl
from jax.experimental.pallas import tpu as pltpu
from jax.sharding import PartitionSpec as P

DH = 128
BLK = 256
EPSILON = 1e-06
KEEP_RATE = 0.75
LONGEST = 8192
F32 = jnp.float32
BF16 = jnp.bfloat16
MESH = pl.DeviceIdType.MESH


def dot(a, b, ca, cb):
    return lax.dot_general(a, b, (((ca,), (cb,)), ((), ())), preferred_element_type=F32)


def same(a, b):
    return jnp.where(a == b, 1.0, 0.0).astype(F32)


def kernel(
    nz, nf, layers, rows, heads,
    q_hbm, k_hbm, v_hbm, g_hbm, gain_hbm, keep_hbm, seg_hbm,
    dq_out, kpart_out, vpart_out, ks_out, vs_out, rq_out, gg_out,
    q_ref, k_ref, v_ref, g_ref, ld_sem, qg_sem, gain_ref, seg_ref, keep_ref, small_sem, out_sem,
    dq_ref, rq_ref, gg_ref,
    segrow, segcol, mask, maskt, mytile, ptile, tabz,
    tails, fronts, cq, qs, qmt, ks, vs, pt, o_ref, do_ref, kpart, vpart,
    dsum, dpart, tot, slots, ebuf, ein, xbuf, dev,
    stat, gain8, gain_sum, gtile, gptile, gslots,
    tile_s, tile_r, tab_s, tab_r,
    d_s, d_r, a_s, a_r, b_r, e_s, e_r, x_s, x_r,
    st_s, st_r, gt_s, gt_r, gz_s, gz_r,
):
    nb = rows // BLK
    cut = DH // nz
    opposite = nz // 2
    reach = min(nz - 1, -(-LONGEST // (2 * rows)))
    steps = sorted(range(1, nz), key=lambda j: -min(j, nz - j))
    features = heads * DH * nf
    s = lax.axis_index("seq")
    f = lax.axis_index("fsdp")
    z = s // 2
    c = s % 2
    partner = (2 * z + 1 - c, f)

    def zmod(x):
        return lax.rem(x + 2 * nz, nz)

    def zpeer(j):
        return (2 * zmod(z + j) + c, f)

    side = math.isqrt(nf)
    others = [(j // side, j % side) for j in range(1, nf)]
    others.sort(key=lambda d: -min(d[0], side - d[0]) - min(d[1], side - d[1]))

    def fpeer(d):
        return (s, lax.rem(f // side + d[0], side) * side + lax.rem(f % side + d[1], side))

    def remote(src, dst, ss, rs, to):
        return pltpu.make_async_remote_copy(
            src_ref=src, dst_ref=dst, send_sem=ss, recv_sem=rs, device_id=to, device_id_type=MESH
        )

    def sent(part, sem):
        remote(part, part, sem, sem, partner).wait_send()

    def arrived(part, sem):
        remote(part, part, sem, sem, partner).wait_recv()

    def load(i, hbm, ref, l):
        return pltpu.make_async_copy(hbm.at[l], ref.at[l], ld_sem.at[i, l])

    small = (
        pltpu.make_async_copy(seg_hbm, seg_ref, small_sem.at[0]),
        pltpu.make_async_copy(gain_hbm, gain_ref, small_sem.at[1]),
        pltpu.make_async_copy(gg_ref, gg_out, small_sem.at[2]),
        pltpu.make_async_copy(keep_hbm, keep_ref, small_sem.at[3]),
    )
    small[0].start()
    load(0, k_hbm, k_ref, 0).start()
    load(1, v_hbm, v_ref, 0).start()
    whole_loads = (
        pltpu.make_async_copy(q_hbm, q_ref, qg_sem.at[0]),
        pltpu.make_async_copy(g_hbm, g_ref, qg_sem.at[1]),
    )

    store_dq, store_k, store_v, store_ks, store_vs, store_rq = (
        pltpu.make_async_copy(ref, out, out_sem.at[i])
        for i, (ref, out) in enumerate((
            (dq_ref, dq_out), (kpart, kpart_out), (vpart, vpart_out),
            (ks, ks_out), (vs, vs_out), (rq_ref, rq_out),
        ))
    )

    barrier = pltpu.get_barrier_semaphore()
    for j in steps:
        pl.semaphore_signal(barrier, inc=1, device_id=zpeer(j), device_id_type=MESH)
    for j in others:
        pl.semaphore_signal(barrier, inc=1, device_id=fpeer(j), device_id_type=MESH)
    pl.semaphore_signal(barrier, inc=1, device_id=partner, device_id_type=MESH)

    small[0].wait()
    for l in range(1, layers):
        load(0, k_hbm, k_ref, l).start()
        load(1, v_hbm, v_ref, l).start()
    seg = seg_ref[...].astype(F32)
    for i in range(rows // 128):
        segrow[0:1, 128 * i : 128 * (i + 1)] = seg[i : i + 1, :]
        segcol[128 * i : 128 * (i + 1), :] = jnp.broadcast_to(seg[i : i + 1, :], (128, 128)).T
    first = [segcol[BLK * b : BLK * b + 1, :] for b in range(nb)]
    last = [segcol[BLK * b + BLK - 1 : BLK * b + BLK, :] for b in range(nb)]
    tile_row = lax.broadcasted_iota(jnp.int32, (8, 128), 0)
    mytile[...] = jnp.where(
        tile_row == 2 * c, first[0], jnp.where(tile_row == 2 * c + 1, last[nb - 1], 0.0)
    )

    def blk(b):
        return slice(BLK * b, BLK * (b + 1))

    def hd(h):
        return slice(DH * h, DH * (h + 1))

    def column_mask(b, value):
        return same(segcol[blk(b), :], value).astype(BF16)

    def wide_mask(b, value):
        return jnp.concatenate([column_mask(b, value)] * heads, axis=1)

    def hand_over(w, l):
        remote(dsum.at[w, l, 1 - c], dpart.at[w, l], d_s.at[w], d_r.at[w, l], partner).start()

    def chip_total(w, l, own_weight, partner_weight):
        arrived(dpart.at[w, l], d_r.at[w, l])
        total = own_weight * dsum[w, l, c] + partner_weight * dpart[w, l]
        tot[w, l] = total
        for j in steps:
            at = pl.multiple_of(zmod(z + j) * cut, cut)
            into = b_r if j == opposite else a_r
            remote(
                tot.at[w, l, pl.ds(at, cut)], slots.at[w, l, z], a_s.at[w], into.at[w, l], zpeer(j)
            ).start()
        slots[w, l, z] = tot[w, l, pl.ds(pl.multiple_of(z * cut, cut), cut)]

    def owner_weights(w):
        row = 3 if w == 0 else 0
        side = -1 if w == 0 else 1
        weights = {}
        for r in range(nz):
            target = zmod(z + r)
            nearest = tabz[zmod(target + side), row : row + 1, :]
            for i in range(1, reach + 1):
                source = target + side * i
                inside = jnp.logical_and(source >= 0, source < nz)
                weight = same(tabz[zmod(source), row : row + 1, :], nearest)
                weights[r, i] = jnp.where(inside, weight, 0.0)
        return weights

    def owner(w, l, weights):
        side = -1 if w == 0 else 1

        def state(r):
            total = None
            for i in range(1, reach + 1):
                term = weights[r, i] * slots[w, l, zmod(z + r + side * i)]
                total = term if total is None else total + term
            return total

        def far_use(r):
            return any((r + side * i - opposite) % nz == 0 for i in range(1, reach + 1))

        here = pl.ds(pl.multiple_of(z * cut, cut), cut)
        arrived(slots.at[w, l, 0 : nz - 2], a_r.at[w, l])
        for late in (False, True):
            if late:
                arrived(slots.at[w, l, 0], b_r.at[w, l])
            for r in steps:
                if far_use(r) == late:
                    ebuf[w, l, zmod(z + r)] = state(r)
                    remote(
                        ebuf.at[w, l, zmod(z + r)], ein.at[w, l, here], e_s.at[w], e_r.at[w, l], zpeer(r)
                    ).start()
        ein[w, l, here] = state(0)

    def entering(w, l, joined):
        arrived(ein.at[w, l, 0 : DH - cut], e_r.at[w, l])
        state = ein[w, l]
        second = c == 1 - w
        own_weight = jnp.where(second, joined, 1.0)
        partner_weight = jnp.where(second, 1.0, joined)
        zero = jnp.zeros((1, DH), F32)
        own_add = jnp.where(second, zero + 1.0, zero)
        partner_add = jnp.where(second, zero, zero + 1.0)
        xbuf[w, l] = partner_weight * state + partner_add * dsum[w, l, c]
        remote(xbuf.at[w, l], dev.at[w, l, c], x_s.at[w], x_r.at[w, l], partner).start()
        dev[w, l, c] = own_weight * state + own_add * dpart[w, l]

    def entered(w, l):
        arrived(dev.at[w, l, 1 - c], x_r.at[w, l])

    def sent_state(w):
        sent(dsum.at[w, :, 0], d_s.at[w])
        sent(tot.at[w, :, 0 : DH - cut], a_s.at[w])
        sent(ebuf.at[w, :, 0 : nz - 1], e_s.at[w])
        sent(xbuf.at[w], x_s.at[w])

    tail_masks = [wide_mask(b, last[b]) for b in range(nb)]
    def tails_of(l, carry):
        load(0, k_hbm, k_ref, l).wait()
        load(1, v_hbm, v_ref, l).wait()
        totals = [None] * heads
        for b in range(nb):
            both = dot(k_ref[l, blk(b), :], v_ref[l, blk(b), :] * tail_masks[b], 0, 0)
            for h in range(heads):
                part = both[hd(h), hd(h)]
                tails[l, h, b] = part
                part = part * same(last[b], last[nb - 1])
                totals[h] = part if totals[h] is None else totals[h] + part
        for h in range(heads):
            dsum[0, l, h] = totals[h]
        return carry

    lax.fori_loop(0, layers, tails_of, 0)
    pl.semaphore_wait(barrier, 1 + (nz - 1) + (nf - 1))
    remote(mytile, ptile, tile_s, tile_r, partner).start()
    for l in range(layers):
        hand_over(0, l)
    for copy in whole_loads:
        copy.start()
    small[1].start()
    small[3].start()

    arrived(ptile, tile_r)
    chiptile = mytile[...] + ptile[...]
    tabz[z] = chiptile
    for j in steps:
        remote(tabz.at[z], tabz.at[z], tab_s, tab_r, zpeer(j)).start()
    first0, last0 = chiptile[0:1], chiptile[1:2]
    first1, last1 = chiptile[2:3], chiptile[3:4]
    is0 = c == 0
    end_own = jnp.where(is0, same(last0, last1), 1.0)
    end_partner = jnp.where(is0, 1.0, same(last0, last1))
    begin_own = jnp.where(is0, 1.0, same(first0, first1))
    begin_partner = jnp.where(is0, same(first0, first1), 1.0)
    for l in range(layers):
        chip_total(0, l, end_own, end_partner)

    at_t = lax.broadcasted_iota(jnp.int32, (BLK, BLK), 0)
    at_s = lax.broadcasted_iota(jnp.int32, (BLK, BLK), 1)
    for b in range(nb):
        wide = jnp.concatenate([segcol[blk(b), :]] * (BLK // 128), axis=1)
        equal = wide == segrow[0:1, blk(b)]
        mask[b] = jnp.where(jnp.logical_and(equal, at_t >= at_s), 1.0, 0.0).astype(BF16)
        maskt[b] = jnp.where(jnp.logical_and(equal, at_s >= at_t), 1.0, 0.0).astype(BF16)

    for l in range(layers):
        for b in range(nb):
            cq[l, b] = jnp.zeros((heads * DH, heads * DH), BF16)
            rq_ref[l, b] = jnp.zeros((heads * DH, heads * DH), BF16)

    whole_loads[0].wait()

    def inner(l, carry):
        for h in range(heads):
            for b in range(nb):
                scores = dot(q_ref[l, blk(b), hd(h)], k_ref[l, blk(b), hd(h)], 1, 1)
                weights = scores.astype(BF16) * mask[b]
                o_ref[l, blk(b), hd(h)] = dot(weights, v_ref[l, blk(b), hd(h)], 1, 0)
        return carry

    lax.fori_loop(0, layers, inner, 0)

    arrived(tabz.at[0 : nz - 1], tab_r)
    weights = owner_weights(0)
    for l in range(layers):
        owner(0, l, weights)

    before_chip = tabz[zmod(z - 1), 3:4, :]
    after_chip = tabz[zmod(z + 1), 0:1, :]
    before = jnp.where(is0, before_chip, last0)
    after = jnp.where(is0, first1, after_chip)
    prior = [before] + last[: nb - 1]
    later = first[1:] + [after]

    def prepare(l, carry):
        for b in range(nb):
            seen_f = column_mask(b, prior[b])
            seen_b = column_mask(b, later[b])
            head = column_mask(b, first[b])
            for h in range(heads):
                q = q_ref[l, blk(b), hd(h)]
                k = k_ref[l, blk(b), hd(h)]
                qs[l, blk(b), hd(h)] = q * seen_f
                qmt[l, hd(h), blk(b)] = (q * head).T
                ks[l, blk(b), hd(h)] = k * seen_b
                vs[l, blk(b), hd(h)] = v_ref[l, blk(b), hd(h)] * seen_b
                pt[l, h, b] = dot(k, q, 1, 1).astype(BF16) * maskt[b]
        return carry

    lax.fori_loop(0, layers, prepare, 0)

    whole_loads[1].wait()
    store_ks.start()
    store_vs.start()
    small[1].wait()
    small[3].wait()
    for l in range(layers):
        gain8[l] = jnp.broadcast_to(gain_ref[l : l + 1, :], (8, heads * DH))
    joined = same(before_chip, last0)

    diagonal = lax.broadcasted_iota(jnp.int32, (128, 128), 0) == lax.broadcasted_iota(jnp.int32, (128, 128), 1)

    def carried(l):
        entered(0, l)
        for h in range(heads):
            state = dev[0, l, h]
            for b in range(nb):
                if b:
                    state = tails[l, h, b - 1] + same(prior[b - 1], prior[b]) * state
                cq[l, b, hd(h), hd(h)] = state.astype(BF16)
        tiles = [[], []]
        for b in range(nb):
            square, cross = None, None
            out = o_ref[l, blk(b), :] + dot(qs[l, blk(b), :], cq[l, b], 1, 0)
            o_ref[l, blk(b), :] = out
            for h in range(heads):
                o = out[:, hd(h)]
                a = g_ref[l, blk(b), hd(h)].astype(F32) * gain8[l, 0:1, hd(h)]
                square = o * o if square is None else square + o * o
                cross = a * o if cross is None else cross + a * o
            for n, x in enumerate((square, cross)):
                total = jnp.sum(x, axis=1, keepdims=True)
                for i in range(BLK // 128):
                    picked = jnp.where(diagonal, total[128 * i : 128 * (i + 1)], 0.0)
                    tiles[n].append(jnp.sum(picked, axis=0, keepdims=True))
        stat[l, f] = jnp.concatenate(tiles[0] + tiles[1], axis=0)
        for j in others:
            remote(stat.at[l, f], stat.at[l, f], st_s, st_r.at[l], fpeer(j)).start()

    for l in range(layers):
        entering(0, l, joined)
        if l > 0:
            carried(l - 1)
    carried(layers - 1)

    def gradient(l, carry):
        arrived(stat.at[l, 0 : nf - 1], st_r.at[l])
        summed = stat[l, 0]
        for i in range(1, nf):
            summed = summed + stat[l, i]
        r = lax.rsqrt(summed[0:8] / features + EPSILON)
        keep = keep_ref[l].astype(F32) / KEEP_RATE
        scale_a = keep * r
        scale_o = scale_a * (r * r) * (summed[8:16] / features)
        turned = jnp.concatenate([scale_a, scale_o, jnp.zeros((112, 128), F32)], axis=0).T
        gains = [jnp.zeros((1, DH), F32) for h in range(heads)]
        totals = [None] * heads
        for b in range(nb):
            per = BLK // 128
            col_a = jnp.concatenate(
                [jnp.broadcast_to(turned[:, per * b + i : per * b + i + 1], (128, 128)) for i in range(per)], axis=0
            )
            col_o = jnp.concatenate(
                [jnp.broadcast_to(turned[:, 8 + per * b + i : 9 + per * b + i], (128, 128)) for i in range(per)], axis=0
            )
            for h in range(heads):
                o = o_ref[l, blk(b), hd(h)]
                up = g_ref[l, blk(b), hd(h)].astype(F32) * col_a
                gains[h] = gains[h] + jnp.sum(up * o, axis=0, keepdims=True)
                grad = (up * gain8[l, 0:1, hd(h)] - o * col_o).astype(BF16)
                do_ref[l, blk(b), hd(h)] = grad
            both = dot(qmt[l, :, blk(b)], do_ref[l, blk(b), :], 1, 0)
            for h in range(heads):
                part = both[hd(h), hd(h)]
                fronts[l, h, b] = part
                part = part * same(first[b], first[0])
                totals[h] = part if totals[h] is None else totals[h] + part
        for h in range(heads):
            dsum[1, l, h] = totals[h]
            gain_sum[l, h] = jnp.broadcast_to(gains[h], (8, DH))
        hand_over(1, l)

        @pl.when(l > 0)
        def _():
            chip_total(1, l - 1, begin_own, begin_partner)

        return carry

    lax.fori_loop(0, layers, gradient, 0)
    for l in range(layers):
        for h in range(heads):
            gtile[heads * l + h : heads * l + h + 1, :] = gain_sum[l, h, 0:1, :]
    for i in range(heads * layers, 8):
        gtile[i : i + 1, :] = jnp.zeros((1, DH), F32)
    remote(gtile, gptile, gt_s, gt_r, partner).start()
    chip_total(1, layers - 1, begin_own, begin_partner)

    def outer_head(l, h):
        for b in range(nb):
            grad = do_ref[l, blk(b), hd(h)]
            v = v_ref[l, blk(b), hd(h)]
            vpart[l, blk(b), hd(h)] = dot(pt[l, h, b], grad, 1, 0)
            gst = dot(v, grad, 1, 1).astype(BF16) * maskt[b]
            kpart[l, blk(b), hd(h)] = dot(gst, q_ref[l, blk(b), hd(h)], 1, 0)

    def outer(l, carry):
        for h in range(heads):
            outer_head(l, h)
        return carry

    lax.fori_loop(0, layers - 2, outer, 0)
    outer_head(layers - 2, 0)
    arrived(gptile, gt_r)
    gslots[z] = gtile[...] + gptile[...]
    for j in steps:
        remote(gslots.at[z], gslots.at[z], gz_s, gz_r, zpeer(j)).start()
    weights = owner_weights(1)
    for l in range(layers - 2):
        owner(1, l, weights)
    for h in range(1, heads):
        outer_head(layers - 2, h)
    owner(1, layers - 2, weights)
    outer_head(layers - 1, 0)
    owner(1, layers - 1, weights)
    for h in range(1, heads):
        outer_head(layers - 1, h)
    store_k.start()
    store_v.start()

    def outer_q(l, carry):
        for b in range(nb):
            carry_part = dot(do_ref[l, blk(b), :] * wide_mask(b, prior[b]), cq[l, b], 1, 1)
            for h in range(heads):
                gs = dot(do_ref[l, blk(b), hd(h)], v_ref[l, blk(b), hd(h)], 1, 1).astype(BF16) * mask[b]
                dq_ref[l, blk(b), hd(h)] = (
                    dot(gs, k_ref[l, blk(b), hd(h)], 1, 0) + carry_part[:, hd(h)]
                ).astype(BF16)
        return carry

    lax.fori_loop(0, layers, outer_q, 0)
    store_dq.start()
    sent(mytile, tile_s)
    sent(tabz.at[0 : nz - 1], tab_s)
    sent_state(0)
    sent(stat.at[:, 0 : nf - 1], st_s)
    sent(gtile, gt_s)

    joined = same(after_chip, first1)
    for l in range(layers):
        entering(1, l, joined)

    arrived(gslots.at[0 : nz - 1], gz_r)
    gtotal = gslots[0]
    for i in range(1, nz):
        gtotal = gtotal + gslots[i]
    for l in range(layers):
        for h in range(heads):
            gg_ref[l : l + 1, hd(h)] = gtotal[heads * l + h : heads * l + h + 1, :]
    small[2].start()
    sent(gslots.at[0 : nz - 1], gz_s)

    for l in range(layers):
        entered(1, l)
        for h in range(heads):
            state = dev[1, l, h]
            for b in range(nb)[::-1]:
                if b < nb - 1:
                    state = fronts[l, h, b + 1] + same(later[b + 1], later[b]) * state
                rq_ref[l, b, hd(h), hd(h)] = state.astype(BF16)
    store_rq.start()
    sent_state(1)
    for copy in (store_ks, store_vs, store_k, store_v, store_dq, small[2], store_rq):
        copy.wait()


def finish(
    layers, rows, heads,
    dq_ref, kpart, vpart, ks, vs, rq, gg_ref,
    dq_hbm, dk_hbm, dv_hbm, gg_hbm,
    dk_ref, dv_ref, sem, gg_sem,
):
    nb = rows // BLK
    gg_copy = pltpu.make_async_copy(gg_ref, gg_hbm, gg_sem)
    gg_copy.start()

    def copy(i, ref, hbm, l):
        return pltpu.make_async_copy(ref.at[l], hbm.at[l], sem.at[i, l])

    for l in range(layers):
        copy(0, dq_ref, dq_hbm, l).start()
    for l in range(layers):
        for b in range(nb):
            at = (l, slice(BLK * b, BLK * (b + 1)))
            dk_ref[at] = (kpart[at] + dot(vs[at], rq[l, b], 1, 1)).astype(BF16)
            dv_ref[at] = (vpart[at] + dot(ks[at], rq[l, b], 1, 0)).astype(BF16)
        copy(1, dk_ref, dk_hbm, l).start()
        copy(2, dv_ref, dv_hbm, l).start()
    gg_copy.wait()
    for l in range(layers):
        copy(0, dq_ref, dq_hbm, l).wait()
        copy(1, dk_ref, dk_hbm, l).wait()
        copy(2, dv_ref, dv_hbm, l).wait()


def local(queries, keys, values, out_grad, gain, keep_mask, segments):
    layers, rows, channels = queries.shape
    heads = channels // DH
    nz = lax.axis_size("seq") // 2
    nf = lax.axis_size("fsdp")
    nb = rows // BLK
    cut = DH // nz
    whole = (layers, rows, channels)
    vmem = pltpu.VMEM
    dma = pltpu.SemaphoreType.DMA
    hbm = pl.BlockSpec(memory_space=pl.ANY)

    def far(x):
        return pltpu.with_memory_space_constraint(x, pltpu.HBM)

    near = pl.BlockSpec(memory_space=pltpu.VMEM)
    scratch = [
        vmem(whole, BF16), vmem(whole, BF16), vmem(whole, BF16), vmem(whole, BF16), dma((2, layers)), dma((2,)),
        vmem((layers, channels), F32), vmem((rows // 128, 128), jnp.int32),
        pltpu.SMEM((layers,), jnp.int32), dma((4,)), dma((6,)),
        vmem(whole, BF16), vmem((layers, nb, channels, channels), BF16), vmem((layers, channels), F32),
        vmem((1, rows), F32), vmem((rows, 128), F32), vmem((nb, BLK, BLK), BF16), vmem((nb, BLK, BLK), BF16),
        vmem((8, 128), F32), vmem((8, 128), F32), vmem((nz, 8, 128), F32),
        vmem((layers, heads, nb, DH, DH), F32), vmem((layers, heads, nb, DH, DH), F32),
        vmem((layers, nb, channels, channels), BF16),
        vmem(whole, BF16), vmem((layers, channels, rows), BF16), vmem(whole, BF16), vmem(whole, BF16),
        vmem((layers, heads, nb, BLK, BLK), BF16),
        vmem(whole, F32), vmem(whole, BF16), vmem(whole, F32), vmem(whole, F32),
        vmem((2, layers, heads, DH, DH), F32), vmem((2, layers, DH, DH), F32), vmem((2, layers, DH, DH), F32),
        vmem((2, layers, nz, cut, DH), F32), vmem((2, layers, nz, cut, DH), F32),
        vmem((2, layers, DH, DH), F32), vmem((2, layers, DH, DH), F32), vmem((2, layers, heads, DH, DH), F32),
        vmem((layers, nf, 16, 128), F32), vmem((layers, 8, channels), F32), vmem((layers, heads, 8, DH), F32),
        vmem((8, 128), F32), vmem((8, 128), F32), vmem((nz, 8, 128), F32),
        dma, dma, dma, dma,
        dma((2,)), dma((2, layers)),
        dma((2,)), dma((2, layers)), dma((2, layers)),
        dma((2,)), dma((2, layers)),
        dma((2,)), dma((2, layers)),
        dma, dma((layers,)),
        dma, dma, dma, dma,
    ]
    results = pl.pallas_call(
        functools.partial(kernel, nz, nf, layers, rows, heads),
        out_shape=(
            vmem(whole, BF16),
            vmem(whole, F32),
            vmem(whole, F32),
            vmem(whole, BF16),
            vmem(whole, BF16),
            vmem((layers, nb, channels, channels), BF16),
            vmem((layers, channels), F32),
        ),
        in_specs=[hbm] * 7,
        out_specs=(hbm,) * 7,
        scratch_shapes=scratch,
        compiler_params=pltpu.CompilerParams(
            collective_id=0, has_side_effects=True, vmem_limit_bytes=44 * 2**20
        ),
        name="backward",
    )(
        far(queries), far(keys), far(values), far(out_grad), far(gain), far(keep_mask),
        far(segments.reshape(rows // 128, 128)),
    )
    return pl.pallas_call(
        functools.partial(finish, layers, rows, heads),
        out_shape=(
            jax.ShapeDtypeStruct(whole, BF16),
            jax.ShapeDtypeStruct(whole, BF16),
            jax.ShapeDtypeStruct(whole, BF16),
            jax.ShapeDtypeStruct((layers, channels), F32),
        ),
        in_specs=[near] * 7,
        out_specs=(hbm,) * 4,
        scratch_shapes=[vmem(whole, BF16), vmem(whole, BF16), dma((3, layers)), dma],
        compiler_params=pltpu.CompilerParams(vmem_limit_bytes=8 * 2**20),
        name="finish",
    )(*[pltpu.with_memory_space_constraint(result, pltpu.VMEM) for result in results])


def solution(mesh):
    wide = P(None, "seq", "fsdp")
    in_specs = (wide, wide, wide, wide, P(None, "fsdp"), P(), P("seq"))
    out_specs = (wide, wide, wide, P(None, "fsdp"))
    return jax.shard_map(local, mesh=mesh, in_specs=in_specs, out_specs=out_specs, check_vma=False)
```

```python
import functools
import math

import jax
import jax.numpy as jnp
from jax import lax
from jax.experimental import pallas as pl
from jax.experimental.pallas import tpu as pltpu
from jax.sharding import PartitionSpec as P

DH = 128
BLK = 256
EPSILON = 1e-06
KEEP_RATE = 0.75
LONGEST = 8192
F32 = jnp.float32
BF16 = jnp.bfloat16
MESH = pl.DeviceIdType.MESH


def dot(a, b, ca, cb):
    return lax.dot_general(a, b, (((ca,), (cb,)), ((), ())), preferred_element_type=F32)


def same(a, b):
    return jnp.where(a == b, 1.0, 0.0).astype(F32)


def kernel(
    nz, nf, layers, rows, heads,
    q_hbm, k_hbm, v_hbm, g_hbm, gain_hbm, keep_hbm, seg_hbm,
    dq_out, kpart_out, vpart_out, ks_out, vs_out, rq_out, gg_out,
    q_ref, k_ref, v_ref, g_ref, ld_sem, qg_sem, gain_ref, seg_ref, keep_ref, small_sem, out_sem,
    dq_ref, rq_ref, gg_ref,
    segrow, segcol, mask, maskt, mytile, ptile, tabz,
    tails, fronts, cq, qs, qmt, ks, vs, pt, o_ref, do_ref, kpart, vpart,
    dsum, dpart, tot, slots, ebuf, ein, xbuf, dev,
    stat, gain8, gain_sum, gtile, gptile, gslots,
    tile_s, tile_r, tab_s, tab_r,
    d_s, d_r, a_s, a_r, b_r, e_s, e_r, x_s, x_r,
    st_s, st_r, gt_s, gt_r, gz_s, gz_r,
):
    nb = rows // BLK
    cut = DH // nz
    opposite = nz // 2
    reach = min(nz - 1, -(-LONGEST // (2 * rows)))
    steps = sorted(range(1, nz), key=lambda j: -min(j, nz - j))
    features = heads * DH * nf
    s = lax.axis_index("seq")
    f = lax.axis_index("fsdp")
    z = s // 2
    c = s % 2
    partner = (2 * z + 1 - c, f)

    def zmod(x):
        return lax.rem(x + 2 * nz, nz)

    def zpeer(j):
        return (2 * zmod(z + j) + c, f)

    side = math.isqrt(nf)
    others = [(j // side, j % side) for j in range(1, nf)]
    others.sort(key=lambda d: -min(d[0], side - d[0]) - min(d[1], side - d[1]))

    def fpeer(d):
        return (s, lax.rem(f // side + d[0], side) * side + lax.rem(f % side + d[1], side))

    def remote(src, dst, ss, rs, to):
        return pltpu.make_async_remote_copy(
            src_ref=src, dst_ref=dst, send_sem=ss, recv_sem=rs, device_id=to, device_id_type=MESH
        )

    def sent(part, sem):
        remote(part, part, sem, sem, partner).wait_send()

    def arrived(part, sem):
        remote(part, part, sem, sem, partner).wait_recv()

    def load(i, hbm, ref, l):
        return pltpu.make_async_copy(hbm.at[l], ref.at[l], ld_sem.at[i, l])

    small = (
        pltpu.make_async_copy(seg_hbm, seg_ref, small_sem.at[0]),
        pltpu.make_async_copy(gain_hbm, gain_ref, small_sem.at[1]),
        pltpu.make_async_copy(gg_ref, gg_out, small_sem.at[2]),
        pltpu.make_async_copy(keep_hbm, keep_ref, small_sem.at[3]),
    )
    small[0].start()
    load(0, k_hbm, k_ref, 0).start()
    load(1, v_hbm, v_ref, 0).start()
    whole_loads = (
        pltpu.make_async_copy(q_hbm, q_ref, qg_sem.at[0]),
        pltpu.make_async_copy(g_hbm, g_ref, qg_sem.at[1]),
    )

    store_dq, store_k, store_v, store_ks, store_vs, store_rq = (
        pltpu.make_async_copy(ref, out, out_sem.at[i])
        for i, (ref, out) in enumerate((
            (dq_ref, dq_out), (kpart, kpart_out), (vpart, vpart_out),
            (ks, ks_out), (vs, vs_out), (rq_ref, rq_out),
        ))
    )

    barrier = pltpu.get_barrier_semaphore()
    for j in steps:
        pl.semaphore_signal(barrier, inc=1, device_id=zpeer(j), device_id_type=MESH)
    for j in others:
        pl.semaphore_signal(barrier, inc=1, device_id=fpeer(j), device_id_type=MESH)
    pl.semaphore_signal(barrier, inc=1, device_id=partner, device_id_type=MESH)

    small[0].wait()
    for l in range(1, layers):
        load(0, k_hbm, k_ref, l).start()
        load(1, v_hbm, v_ref, l).start()
    seg = seg_ref[...].astype(F32)
    for i in range(rows // 128):
        segrow[0:1, 128 * i : 128 * (i + 1)] = seg[i : i + 1, :]
        segcol[128 * i : 128 * (i + 1), :] = jnp.broadcast_to(seg[i : i + 1, :], (128, 128)).T
    first = [segcol[BLK * b : BLK * b + 1, :] for b in range(nb)]
    last = [segcol[BLK * b + BLK - 1 : BLK * b + BLK, :] for b in range(nb)]
    tile_row = lax.broadcasted_iota(jnp.int32, (8, 128), 0)
    mytile[...] = jnp.where(
        tile_row == 2 * c, first[0], jnp.where(tile_row == 2 * c + 1, last[nb - 1], 0.0)
    )

    def blk(b):
        return slice(BLK * b, BLK * (b + 1))

    def hd(h):
        return slice(DH * h, DH * (h + 1))

    def column_mask(b, value):
        return same(segcol[blk(b), :], value).astype(BF16)

    def wide_mask(b, value):
        return jnp.concatenate([column_mask(b, value)] * heads, axis=1)

    def hand_over(w, l):
        remote(dsum.at[w, l, 1 - c], dpart.at[w, l], d_s.at[w], d_r.at[w, l], partner).start()

    def chip_total(w, l, own_weight, partner_weight):
        arrived(dpart.at[w, l], d_r.at[w, l])
        total = own_weight * dsum[w, l, c] + partner_weight * dpart[w, l]
        tot[w, l] = total
        for j in steps:
            at = pl.multiple_of(zmod(z + j) * cut, cut)
            into = b_r if j == opposite else a_r
            remote(
                tot.at[w, l, pl.ds(at, cut)], slots.at[w, l, z], a_s.at[w], into.at[w, l], zpeer(j)
            ).start()
        slots[w, l, z] = tot[w, l, pl.ds(pl.multiple_of(z * cut, cut), cut)]

    def owner_weights(w):
        row = 1 if w == 0 else 0
        side = -1 if w == 0 else 1
        weights = {}
        for r in range(nz):
            target = zmod(z + r)
            nearest = tabz[zmod(target + side), row : row + 1, :]
            for i in range(1, reach + 1):
                source = target + side * i
                inside = jnp.logical_and(source >= 0, source < nz)
                weight = same(tabz[zmod(source), row : row + 1, :], nearest)
                weights[r, i] = jnp.where(inside, weight, 0.0)
        return weights

    def owner(w, l, weights):
        side = -1 if w == 0 else 1

        def state(r):
            total = None
            for i in range(1, reach + 1):
                term = weights[r, i] * slots[w, l, zmod(z + r + side * i)]
                total = term if total is None else total + term
            return total

        def far_use(r):
            return any((r + side * i - opposite) % nz == 0 for i in range(1, reach + 1))

        here = pl.ds(pl.multiple_of(z * cut, cut), cut)
        arrived(slots.at[w, l, 0 : nz - 2], a_r.at[w, l])
        for late in (False, True):
            if late:
                arrived(slots.at[w, l, 0], b_r.at[w, l])
            for r in steps:
                if far_use(r) == late:
                    ebuf[w, l, zmod(z + r)] = state(r)
                    remote(
                        ebuf.at[w, l, zmod(z + r)], ein.at[w, l, here], e_s.at[w], e_r.at[w, l], zpeer(r)
                    ).start()
        ein[w, l, here] = state(0)

    def entering(w, l, joined):
        arrived(ein.at[w, l, 0 : DH - cut], e_r.at[w, l])
        state = ein[w, l]
        second = c == 1 - w
        own_weight = jnp.where(second, joined, 1.0)
        partner_weight = jnp.where(second, 1.0, joined)
        zero = jnp.zeros((1, DH), F32)
        own_add = jnp.where(second, zero + 1.0, zero)
        partner_add = jnp.where(second, zero, zero + 1.0)
        xbuf[w, l] = partner_weight * state + partner_add * dsum[w, l, c]
        remote(xbuf.at[w, l], dev.at[w, l, c], x_s.at[w], x_r.at[w, l], partner).start()
        dev[w, l, c] = own_weight * state + own_add * dpart[w, l]

    def entered(w, l):
        arrived(dev.at[w, l, 1 - c], x_r.at[w, l])

    def sent_state(w):
        sent(dsum.at[w, :, 0], d_s.at[w])
        sent(tot.at[w, :, 0 : DH - cut], a_s.at[w])
        sent(ebuf.at[w, :, 0 : nz - 1], e_s.at[w])
        sent(xbuf.at[w], x_s.at[w])

    tail_masks = [wide_mask(b, last[b]) for b in range(nb)]
    def tails_of(l, carry):
        load(0, k_hbm, k_ref, l).wait()
        load(1, v_hbm, v_ref, l).wait()
        totals = [None] * heads
        for b in range(nb):
            both = dot(k_ref[l, blk(b), :], v_ref[l, blk(b), :] * tail_masks[b], 0, 0)
            for h in range(heads):
                part = both[hd(h), hd(h)]
                tails[l, h, b] = part
                part = part * same(last[b], last[nb - 1])
                totals[h] = part if totals[h] is None else totals[h] + part
        for h in range(heads):
            dsum[0, l, h] = totals[h]
        return carry

    lax.fori_loop(0, layers, tails_of, 0)
    pl.semaphore_wait(barrier, 1 + (nz - 1) + (nf - 1))
    remote(mytile, ptile, tile_s, tile_r, partner).start()
    for l in range(layers):
        hand_over(0, l)
    for copy in whole_loads:
        copy.start()
    small[1].start()
    small[3].start()

    arrived(ptile, tile_r)
    chiptile = mytile[...] + ptile[...]
    tabz[z] = jnp.concatenate([chiptile[0:1], chiptile[3:4]], axis=0)
    for j in steps:
        remote(tabz.at[z], tabz.at[z], tab_s, tab_r, zpeer(j)).start()
    first0, last0 = chiptile[0:1], chiptile[1:2]
    first1, last1 = chiptile[2:3], chiptile[3:4]
    is0 = c == 0
    end_own = jnp.where(is0, same(last0, last1), 1.0)
    end_partner = jnp.where(is0, 1.0, same(last0, last1))
    begin_own = jnp.where(is0, 1.0, same(first0, first1))
    begin_partner = jnp.where(is0, same(first0, first1), 1.0)
    for l in range(layers):
        chip_total(0, l, end_own, end_partner)

    at_t = lax.broadcasted_iota(jnp.int32, (BLK, BLK), 0)
    at_s = lax.broadcasted_iota(jnp.int32, (BLK, BLK), 1)
    for b in range(nb):
        wide = jnp.concatenate([segcol[blk(b), :]] * (BLK // 128), axis=1)
        equal = wide == segrow[0:1, blk(b)]
        mask[b] = jnp.where(jnp.logical_and(equal, at_t >= at_s), 1.0, 0.0).astype(BF16)
        maskt[b] = jnp.where(jnp.logical_and(equal, at_s >= at_t), 1.0, 0.0).astype(BF16)

    for l in range(layers):
        for b in range(nb):
            cq[l, b] = jnp.zeros((heads * DH, heads * DH), BF16)

    whole_loads[0].wait()

    def inner(l, carry):
        for h in range(heads):
            for b in range(nb):
                scores = dot(q_ref[l, blk(b), hd(h)], k_ref[l, blk(b), hd(h)], 1, 1)
                weights = scores.astype(BF16) * mask[b]
                o_ref[l, blk(b), hd(h)] = dot(weights, v_ref[l, blk(b), hd(h)], 1, 0)
        return carry

    lax.fori_loop(0, layers, inner, 0)

    def prepare(l, carry):
        for b in range(nb):
            qmt[l, :, blk(b)] = (q_ref[l, blk(b), :] * wide_mask(b, first[b])).T
            for h in range(heads):
                pt[l, h, b] = (
                    dot(k_ref[l, blk(b), hd(h)], q_ref[l, blk(b), hd(h)], 1, 1).astype(BF16) * maskt[b]
                )
        return carry

    lax.fori_loop(0, layers, prepare, 0)

    arrived(tabz.at[0 : nz - 1], tab_r)
    weights = owner_weights(0)
    for l in range(layers):
        owner(0, l, weights)

    before_chip = tabz[zmod(z - 1), 1:2, :]
    after_chip = tabz[zmod(z + 1), 0:1, :]
    before = jnp.where(is0, before_chip, last0)
    after = jnp.where(is0, first1, after_chip)
    prior = [before] + last[: nb - 1]
    later = first[1:] + [after]

    def select(l, carry):
        for b in range(nb):
            qs[l, blk(b), :] = q_ref[l, blk(b), :] * wide_mask(b, prior[b])
            seen_b = wide_mask(b, later[b])
            ks[l, blk(b), :] = k_ref[l, blk(b), :] * seen_b
            vs[l, blk(b), :] = v_ref[l, blk(b), :] * seen_b
        return carry

    lax.fori_loop(0, layers, select, 0)
    whole_loads[1].wait()
    store_ks.start()
    store_vs.start()
    small[1].wait()
    small[3].wait()
    for l in range(layers):
        gain8[l] = jnp.broadcast_to(gain_ref[l : l + 1, :], (8, heads * DH))
    joined = same(before_chip, last0)

    diagonal = lax.broadcasted_iota(jnp.int32, (128, 128), 0) == lax.broadcasted_iota(jnp.int32, (128, 128), 1)

    def carried(l):
        entered(0, l)
        for h in range(heads):
            state = dev[0, l, h]
            for b in range(nb):
                if b:
                    state = tails[l, h, b - 1] + same(prior[b - 1], prior[b]) * state
                cq[l, b, hd(h), hd(h)] = state.astype(BF16)
        tiles = [[], []]
        for b in range(nb):
            square, cross = None, None
            out = o_ref[l, blk(b), :] + dot(qs[l, blk(b), :], cq[l, b], 1, 0)
            o_ref[l, blk(b), :] = out
            for h in range(heads):
                o = out[:, hd(h)]
                a = g_ref[l, blk(b), hd(h)].astype(F32) * gain8[l, 0:1, hd(h)]
                square = o * o if square is None else square + o * o
                cross = a * o if cross is None else cross + a * o
            for n, x in enumerate((square, cross)):
                total = jnp.sum(x, axis=1, keepdims=True)
                for i in range(BLK // 128):
                    picked = jnp.where(diagonal, total[128 * i : 128 * (i + 1)], 0.0)
                    tiles[n].append(jnp.sum(picked, axis=0, keepdims=True))
        stat[l, f] = jnp.concatenate(tiles[0] + tiles[1], axis=0)
        for j in others:
            remote(stat.at[l, f], stat.at[l, f], st_s, st_r.at[l], fpeer(j)).start()

    for l in range(layers):
        entering(0, l, joined)
        if l > 0:
            carried(l - 1)
    carried(layers - 1)

    def gradient(l, carry):
        arrived(stat.at[l, 0 : nf - 1], st_r.at[l])
        summed = stat[l, 0]
        for i in range(1, nf):
            summed = summed + stat[l, i]
        r = lax.rsqrt(summed[0:8] / features + EPSILON)
        keep = keep_ref[l].astype(F32) / KEEP_RATE
        scale_a = keep * r
        scale_o = scale_a * (r * r) * (summed[8:16] / features)
        turned = jnp.concatenate([scale_a, scale_o, jnp.zeros((112, 128), F32)], axis=0).T
        gains = [jnp.zeros((1, DH), F32) for h in range(heads)]
        totals = [None] * heads
        for b in range(nb):
            per = BLK // 128
            col_a = jnp.concatenate(
                [jnp.broadcast_to(turned[:, per * b + i : per * b + i + 1], (128, 128)) for i in range(per)], axis=0
            )
            col_o = jnp.concatenate(
                [jnp.broadcast_to(turned[:, 8 + per * b + i : 9 + per * b + i], (128, 128)) for i in range(per)], axis=0
            )
            for h in range(heads):
                o = o_ref[l, blk(b), hd(h)]
                up = g_ref[l, blk(b), hd(h)].astype(F32) * col_a
                gains[h] = gains[h] + jnp.sum(up * o, axis=0, keepdims=True)
                grad = (up * gain8[l, 0:1, hd(h)] - o * col_o).astype(BF16)
                do_ref[l, blk(b), hd(h)] = grad
            both = dot(qmt[l, :, blk(b)], do_ref[l, blk(b), :], 1, 0)
            for h in range(heads):
                part = both[hd(h), hd(h)]
                fronts[l, h, b] = part
                part = part * same(first[b], first[0])
                totals[h] = part if totals[h] is None else totals[h] + part
        for h in range(heads):
            dsum[1, l, h] = totals[h]
            gain_sum[l, h] = jnp.broadcast_to(gains[h], (8, DH))
        hand_over(1, l)

        @pl.when(l > 0)
        def _():
            chip_total(1, l - 1, begin_own, begin_partner)

        return carry

    lax.fori_loop(0, layers, gradient, 0)
    for l in range(layers):
        for h in range(heads):
            gtile[heads * l + h : heads * l + h + 1, :] = gain_sum[l, h, 0:1, :]
    for i in range(heads * layers, 8):
        gtile[i : i + 1, :] = jnp.zeros((1, DH), F32)
    remote(gtile, gptile, gt_s, gt_r, partner).start()
    chip_total(1, layers - 1, begin_own, begin_partner)

    def outer_head(l, h):
        for b in range(nb):
            grad = do_ref[l, blk(b), hd(h)]
            v = v_ref[l, blk(b), hd(h)]
            vpart[l, blk(b), hd(h)] = dot(pt[l, h, b], grad, 1, 0)
            gst = dot(v, grad, 1, 1).astype(BF16) * maskt[b]
            kpart[l, blk(b), hd(h)] = dot(gst, q_ref[l, blk(b), hd(h)], 1, 0)

    def outer(l, carry):
        for h in range(heads):
            outer_head(l, h)
        return carry

    def outer_q(l, carry):
        for b in range(nb):
            carry_part = dot(do_ref[l, blk(b), :] * wide_mask(b, prior[b]), cq[l, b], 1, 1)
            for h in range(heads):
                gs = dot(do_ref[l, blk(b), hd(h)], v_ref[l, blk(b), hd(h)], 1, 1).astype(BF16) * mask[b]
                dq_ref[l, blk(b), hd(h)] = (
                    dot(gs, k_ref[l, blk(b), hd(h)], 1, 0) + carry_part[:, hd(h)]
                ).astype(BF16)
        return carry

    lax.fori_loop(0, layers - 2, outer, 0)
    outer_q(0, 0)
    arrived(gptile, gt_r)
    gslots[z] = gtile[...] + gptile[...]
    weights = owner_weights(1)
    for l in range(layers - 2):
        owner(1, l, weights)
    outer_head(layers - 2, 0)
    owner(1, layers - 2, weights)
    for h in range(1, heads):
        outer_head(layers - 2, h)
    owner(1, layers - 1, weights)
    for j in steps:
        remote(gslots.at[z], gslots.at[z], gz_s, gz_r, zpeer(j)).start()
    lax.fori_loop(layers - 1, layers, outer, 0)
    store_k.start()
    store_v.start()

    def later_states(l):
        entered(1, l)
        for h in range(heads):
            state = dev[1, l, h]
            for b in range(nb)[::-1]:
                if b < nb - 1:
                    state = fronts[l, h, b + 1] + same(later[b + 1], later[b]) * state
                rq_ref[l, h, b] = state.astype(BF16)
        pltpu.make_async_copy(rq_ref.at[l], rq_out.at[l], out_sem.at[5]).start()

    joined = same(after_chip, first1)
    for l in range(1, layers):
        outer_q(l, 0)
        entering(1, l - 1, joined)
    store_dq.start()
    sent(mytile, tile_s)
    sent(tabz.at[0 : nz - 1], tab_s)
    sent_state(0)
    sent(stat.at[:, 0 : nf - 1], st_s)
    sent(gtile, gt_s)

    for l in range(layers - 2):
        later_states(l)
    entering(1, layers - 1, joined)
    for l in range(max(0, layers - 2), layers):
        later_states(l)
    arrived(gslots.at[0 : nz - 1], gz_r)
    gtotal = gslots[0]
    for i in range(1, nz):
        gtotal = gtotal + gslots[i]
    for l in range(layers):
        for h in range(heads):
            gg_ref[l : l + 1, hd(h)] = gtotal[heads * l + h : heads * l + h + 1, :]
    small[2].start()
    sent(gslots.at[0 : nz - 1], gz_s)
    sent_state(1)
    for copy in (store_ks, store_vs, store_k, store_v, store_dq, small[2], store_rq):
        copy.wait()


def finish(
    layers, rows, heads,
    dq_ref, kpart, vpart, ks, vs, rq, gg_ref,
    dq_hbm, dk_hbm, dv_hbm, gg_hbm,
    dk_ref, dv_ref, sem, gg_sem,
):
    nb = rows // BLK
    gg_copy = pltpu.make_async_copy(gg_ref, gg_hbm, gg_sem)
    gg_copy.start()

    def copy(i, ref, hbm, l):
        return pltpu.make_async_copy(ref.at[l], hbm.at[l], sem.at[i, l])

    for l in range(layers):
        copy(0, dq_ref, dq_hbm, l).start()
    for l in range(layers):
        for b in range(nb):
            for h in range(heads):
                at = (l, slice(BLK * b, BLK * (b + 1)), slice(DH * h, DH * (h + 1)))
                dk_ref[at] = (kpart[at] + dot(vs[at], rq[l, h, b], 1, 1)).astype(BF16)
                dv_ref[at] = (vpart[at] + dot(ks[at], rq[l, h, b], 1, 0)).astype(BF16)
        copy(1, dk_ref, dk_hbm, l).start()
        copy(2, dv_ref, dv_hbm, l).start()
    gg_copy.wait()
    for l in range(layers):
        copy(0, dq_ref, dq_hbm, l).wait()
        copy(1, dk_ref, dk_hbm, l).wait()
        copy(2, dv_ref, dv_hbm, l).wait()


def local(queries, keys, values, out_grad, gain, keep_mask, segments):
    layers, rows, channels = queries.shape
    heads = channels // DH
    nz = lax.axis_size("seq") // 2
    nf = lax.axis_size("fsdp")
    nb = rows // BLK
    cut = DH // nz
    whole = (layers, rows, channels)
    vmem = pltpu.VMEM
    dma = pltpu.SemaphoreType.DMA
    hbm = pl.BlockSpec(memory_space=pl.ANY)

    def far(x):
        return pltpu.with_memory_space_constraint(x, pltpu.HBM)

    near = pl.BlockSpec(memory_space=pltpu.VMEM)
    scratch = [
        vmem(whole, BF16), vmem(whole, BF16), vmem(whole, BF16), vmem(whole, BF16), dma((2, layers)), dma((2,)),
        vmem((layers, channels), F32), vmem((rows // 128, 128), jnp.int32),
        pltpu.SMEM((layers,), jnp.int32), dma((4,)), dma((6,)),
        vmem(whole, BF16), vmem((layers, heads, nb, DH, DH), BF16), vmem((layers, channels), F32),
        vmem((1, rows), F32), vmem((rows, 128), F32), vmem((nb, BLK, BLK), BF16), vmem((nb, BLK, BLK), BF16),
        vmem((8, 128), F32), vmem((8, 128), F32), vmem((nz, 2, 128), F32),
        vmem((layers, heads, nb, DH, DH), F32), vmem((layers, heads, nb, DH, DH), F32),
        vmem((layers, nb, channels, channels), BF16),
        vmem(whole, BF16), vmem((layers, channels, rows), BF16), vmem(whole, BF16), vmem(whole, BF16),
        vmem((layers, heads, nb, BLK, BLK), BF16),
        vmem(whole, F32), vmem(whole, BF16), vmem(whole, F32), vmem(whole, F32),
        vmem((2, layers, heads, DH, DH), F32), vmem((2, layers, DH, DH), F32), vmem((2, layers, DH, DH), F32),
        vmem((2, layers, nz, cut, DH), F32), vmem((2, layers, nz, cut, DH), F32),
        vmem((2, layers, DH, DH), F32), vmem((2, layers, DH, DH), F32), vmem((2, layers, heads, DH, DH), F32),
        vmem((layers, nf, 16, 128), F32), vmem((layers, 8, channels), F32), vmem((layers, heads, 8, DH), F32),
        vmem((8, 128), F32), vmem((8, 128), F32), vmem((nz, 8, 128), F32),
        dma, dma, dma, dma,
        dma((2,)), dma((2, layers)),
        dma((2,)), dma((2, layers)), dma((2, layers)),
        dma((2,)), dma((2, layers)),
        dma((2,)), dma((2, layers)),
        dma, dma((layers,)),
        dma, dma, dma, dma,
    ]
    results = pl.pallas_call(
        functools.partial(kernel, nz, nf, layers, rows, heads),
        out_shape=(
            vmem(whole, BF16),
            vmem(whole, F32),
            vmem(whole, F32),
            vmem(whole, BF16),
            vmem(whole, BF16),
            vmem((layers, heads, nb, DH, DH), BF16),
            vmem((layers, channels), F32),
        ),
        in_specs=[hbm] * 7,
        out_specs=(hbm,) * 7,
        scratch_shapes=scratch,
        compiler_params=pltpu.CompilerParams(
            collective_id=0, has_side_effects=True, vmem_limit_bytes=44 * 2**20
        ),
        name="backward",
    )(
        far(queries), far(keys), far(values), far(out_grad), far(gain), far(keep_mask),
        far(segments.reshape(rows // 128, 128)),
    )
    return pl.pallas_call(
        functools.partial(finish, layers, rows, heads),
        out_shape=(
            jax.ShapeDtypeStruct(whole, BF16),
            jax.ShapeDtypeStruct(whole, BF16),
            jax.ShapeDtypeStruct(whole, BF16),
            jax.ShapeDtypeStruct((layers, channels), F32),
        ),
        in_specs=[near] * 7,
        out_specs=(hbm,) * 4,
        scratch_shapes=[vmem(whole, BF16), vmem(whole, BF16), dma((3, layers)), dma],
        compiler_params=pltpu.CompilerParams(vmem_limit_bytes=8 * 2**20),
        name="finish",
    )(*[pltpu.with_memory_space_constraint(result, pltpu.VMEM) for result in results])


def solution(mesh):
    wide = P(None, "seq", "fsdp")
    in_specs = (wide, wide, wide, wide, P(None, "fsdp"), P(), P("seq"))
    out_specs = (wide, wide, wide, P(None, "fsdp"))
    return jax.shard_map(local, mesh=mesh, in_specs=in_specs, out_specs=out_specs, check_vma=False)
```

```python
import functools
import math

import jax
import jax.numpy as jnp
from jax import lax
from jax.experimental import pallas as pl
from jax.experimental.pallas import tpu as pltpu
from jax.sharding import PartitionSpec as P

DH = 128
BLK = 256
EPSILON = 1e-06
KEEP_RATE = 0.75
LONGEST = 8192
F32 = jnp.float32
BF16 = jnp.bfloat16
MESH = pl.DeviceIdType.MESH


def dot(a, b, ca, cb):
    return lax.dot_general(a, b, (((ca,), (cb,)), ((), ())), preferred_element_type=F32)


def same(a, b):
    return jnp.where(a == b, 1.0, 0.0).astype(F32)


def kernel(
    nz, nf, layers, rows, heads,
    q_hbm, k_hbm, v_hbm, g_hbm, gain_hbm, keep_hbm, seg_hbm,
    dq_out, kpart_out, vpart_out, ks_out, vs_out, rq_out, gg_out,
    q_ref, k_ref, v_ref, g_ref, ld_sem, qg_sem, gain_ref, seg_ref, keep_ref, small_sem, out_sem,
    dq_ref, rq_ref, gg_ref,
    segrow, segcol, mask, maskt, mytile, ptile, tabz,
    tails, fronts, cq, qs, qmt, ks, vs, pt, o_ref, do_ref, kpart, vpart,
    dsum, dpart, tot, slots, ebuf, ein, xbuf, dev,
    stat, gain8, gain_sum, gtile, gptile, gslots,
    tile_s, tile_r, tab_s, tab_r,
    d_s, d_r, a_s, a_r, b_r, e_s, e_r, x_s, x_r,
    st_s, st_r, gt_s, gt_r, gz_s, gz_r,
):
    nb = rows // BLK
    cut = DH // nz
    opposite = nz // 2
    reach = min(nz - 1, -(-LONGEST // (2 * rows)))
    steps = sorted(range(1, nz), key=lambda j: -min(j, nz - j))
    features = heads * DH * nf
    s = lax.axis_index("seq")
    f = lax.axis_index("fsdp")
    z = s // 2
    c = s % 2
    partner = (2 * z + 1 - c, f)

    def zmod(x):
        return lax.rem(x + 2 * nz, nz)

    def zpeer(j):
        return (2 * zmod(z + j) + c, f)

    side = math.isqrt(nf)
    others = [(j // side, j % side) for j in range(1, nf)]
    others.sort(key=lambda d: -min(d[0], side - d[0]) - min(d[1], side - d[1]))

    def fpeer(d):
        return (s, lax.rem(f // side + d[0], side) * side + lax.rem(f % side + d[1], side))

    def remote(src, dst, ss, rs, to):
        return pltpu.make_async_remote_copy(
            src_ref=src, dst_ref=dst, send_sem=ss, recv_sem=rs, device_id=to, device_id_type=MESH
        )

    def sent(part, sem):
        remote(part, part, sem, sem, partner).wait_send()

    def arrived(part, sem):
        remote(part, part, sem, sem, partner).wait_recv()

    def load(i, hbm, ref, l):
        return pltpu.make_async_copy(hbm.at[l], ref.at[l], ld_sem.at[l])

    small = (
        pltpu.make_async_copy(seg_hbm, seg_ref, small_sem.at[0]),
        pltpu.make_async_copy(gain_hbm, gain_ref, small_sem.at[1]),
        pltpu.make_async_copy(gg_ref, gg_out, small_sem.at[2]),
        pltpu.make_async_copy(keep_hbm, keep_ref, small_sem.at[3]),
    )
    small[0].start()
    load(0, k_hbm, k_ref, 0).start()
    load(1, v_hbm, v_ref, 0).start()
    whole_loads = (
        pltpu.make_async_copy(q_hbm, q_ref, qg_sem.at[0]),
        pltpu.make_async_copy(g_hbm, g_ref, qg_sem.at[1]),
    )

    store_dq, store_k, store_v, store_ks, store_vs, store_rq = (
        pltpu.make_async_copy(ref, out, out_sem.at[i])
        for i, (ref, out) in enumerate((
            (dq_ref, dq_out), (kpart, kpart_out), (vpart, vpart_out),
            (ks, ks_out), (vs, vs_out), (rq_ref, rq_out),
        ))
    )

    barrier = pltpu.get_barrier_semaphore()
    for j in steps:
        pl.semaphore_signal(barrier, inc=1, device_id=zpeer(j), device_id_type=MESH)
    for j in others:
        pl.semaphore_signal(barrier, inc=1, device_id=fpeer(j), device_id_type=MESH)
    pl.semaphore_signal(barrier, inc=1, device_id=partner, device_id_type=MESH)

    small[0].wait()
    for l in range(1, layers):
        load(0, k_hbm, k_ref, l).start()
        load(1, v_hbm, v_ref, l).start()
    seg = seg_ref[...].astype(F32)
    for i in range(rows // 128):
        segrow[0:1, 128 * i : 128 * (i + 1)] = seg[i : i + 1, :]
        segcol[128 * i : 128 * (i + 1), :] = jnp.broadcast_to(seg[i : i + 1, :], (128, 128)).T
    first = [segcol[BLK * b : BLK * b + 1, :] for b in range(nb)]
    last = [segcol[BLK * b + BLK - 1 : BLK * b + BLK, :] for b in range(nb)]
    tile_row = lax.broadcasted_iota(jnp.int32, (8, 128), 0)
    mytile[...] = jnp.where(
        tile_row == 2 * c, first[0], jnp.where(tile_row == 2 * c + 1, last[nb - 1], 0.0)
    )

    def blk(b):
        return slice(BLK * b, BLK * (b + 1))

    def hd(h):
        return slice(DH * h, DH * (h + 1))

    def column_mask(b, value):
        return same(segcol[blk(b), :], value).astype(BF16)

    def wide_mask(b, value):
        return jnp.concatenate([column_mask(b, value)] * heads, axis=1)

    def hand_over(w, l):
        remote(dsum.at[w, l, 1 - c], dpart.at[w, l], d_s, d_r.at[w, l], partner).start()

    def chip_total(w, l, own_weight, partner_weight):
        arrived(dpart.at[w, l], d_r.at[w, l])
        total = own_weight * dsum[w, l, c] + partner_weight * dpart[w, l]
        tot[w, l] = total
        for j in steps:
            at = pl.multiple_of(zmod(z + j) * cut, cut)
            into = b_r if j == opposite else a_r
            remote(
                tot.at[w, l, pl.ds(at, cut)], slots.at[w, l, z], a_s, into.at[w, l], zpeer(j)
            ).start()
        slots[w, l, z] = tot[w, l, pl.ds(pl.multiple_of(z * cut, cut), cut)]

    def owner_weights(w):
        row = 1 if w == 0 else 0
        side = -1 if w == 0 else 1
        weights = {}
        for r in range(nz):
            target = zmod(z + r)
            nearest = tabz[zmod(target + side), row : row + 1, :]
            for i in range(1, reach + 1):
                source = target + side * i
                inside = jnp.logical_and(source >= 0, source < nz)
                weight = same(tabz[zmod(source), row : row + 1, :], nearest)
                weights[r, i] = jnp.where(inside, weight, 0.0)
        return weights

    def owner(w, l, weights):
        side = -1 if w == 0 else 1

        def state(r):
            total = None
            for i in range(1, reach + 1):
                term = weights[r, i] * slots[w, l, zmod(z + r + side * i)]
                total = term if total is None else total + term
            return total

        def far_use(r):
            return any((r + side * i - opposite) % nz == 0 for i in range(1, reach + 1))

        here = pl.ds(pl.multiple_of(z * cut, cut), cut)
        arrived(slots.at[w, l, 0 : nz - 2], a_r.at[w, l])
        for late in (False, True):
            if late:
                arrived(slots.at[w, l, 0], b_r.at[w, l])
            for r in steps:
                if far_use(r) == late:
                    ebuf[w, l, zmod(z + r)] = state(r)
                    remote(
                        ebuf.at[w, l, zmod(z + r)], ein.at[w, l, here], e_s, e_r.at[w, l], zpeer(r)
                    ).start()
        ein[w, l, here] = state(0)

    def entering(w, l, joined):
        arrived(ein.at[w, l, 0 : DH - cut], e_r.at[w, l])
        state = ein[w, l]
        second = c == 1 - w
        own_weight = jnp.where(second, joined, 1.0)
        partner_weight = jnp.where(second, 1.0, joined)
        zero = jnp.zeros((1, DH), F32)
        own_add = jnp.where(second, zero + 1.0, zero)
        partner_add = jnp.where(second, zero, zero + 1.0)
        xbuf[w, l] = partner_weight * state + partner_add * dsum[w, l, c]
        remote(xbuf.at[w, l], dev.at[w, l, c], x_s, x_r.at[w, l], partner).start()
        dev[w, l, c] = own_weight * state + own_add * dpart[w, l]

    def entered(w, l):
        arrived(dev.at[w, l, 1 - c], x_r.at[w, l])

    def sent_state(w):
        sent(dsum.at[w, :, 0], d_s)
        sent(tot.at[w, :, 0 : DH - cut], a_s)
        sent(ebuf.at[w, :, 0 : nz - 1], e_s)
        sent(xbuf.at[w], x_s)

    tail_masks = [wide_mask(b, last[b]) for b in range(nb)]
    def tails_of(l, carry):
        pltpu.make_async_copy(k_hbm.at[0:2], k_ref.at[0:2], ld_sem.at[l]).wait()
        totals = [None] * heads
        for b in range(nb):
            both = dot(k_ref[l, blk(b), :], v_ref[l, blk(b), :] * tail_masks[b], 0, 0)
            for h in range(heads):
                part = both[hd(h), hd(h)]
                tails[l, h, b] = part
                part = part * same(last[b], last[nb - 1])
                totals[h] = part if totals[h] is None else totals[h] + part
        for h in range(heads):
            dsum[0, l, h] = totals[h]
        return carry

    lax.fori_loop(0, layers, tails_of, 0)
    pl.semaphore_wait(barrier, 1 + (nz - 1) + (nf - 1))
    remote(mytile, ptile, tile_s, tile_r, partner).start()
    for l in range(layers):
        hand_over(0, l)
    for copy in whole_loads:
        copy.start()
    small[1].start()
    small[3].start()

    arrived(ptile, tile_r)
    chiptile = mytile[...] + ptile[...]
    tabz[z] = jnp.concatenate([chiptile[0:1], chiptile[3:4]], axis=0)
    for j in steps:
        remote(tabz.at[z], tabz.at[z], tab_s, tab_r, zpeer(j)).start()
    first0, last0 = chiptile[0:1], chiptile[1:2]
    first1, last1 = chiptile[2:3], chiptile[3:4]
    is0 = c == 0
    end_own = jnp.where(is0, same(last0, last1), 1.0)
    end_partner = jnp.where(is0, 1.0, same(last0, last1))
    begin_own = jnp.where(is0, 1.0, same(first0, first1))
    begin_partner = jnp.where(is0, same(first0, first1), 1.0)
    for l in range(layers):
        chip_total(0, l, end_own, end_partner)

    at_t = lax.broadcasted_iota(jnp.int32, (BLK, BLK), 0)
    at_s = lax.broadcasted_iota(jnp.int32, (BLK, BLK), 1)
    for b in range(nb):
        wide = jnp.concatenate([segcol[blk(b), :]] * (BLK // 128), axis=1)
        equal = wide == segrow[0:1, blk(b)]
        mask[b] = jnp.where(jnp.logical_and(equal, at_t >= at_s), 1.0, 0.0).astype(BF16)
        maskt[b] = jnp.where(jnp.logical_and(equal, at_s >= at_t), 1.0, 0.0).astype(BF16)

    for l in range(layers):
        for b in range(nb):
            cq[l, b] = jnp.zeros((heads * DH, heads * DH), BF16)

    whole_loads[0].wait()

    def inner(l, carry):
        for h in range(heads):
            for b in range(nb):
                scores = dot(q_ref[l, blk(b), hd(h)], k_ref[l, blk(b), hd(h)], 1, 1)
                weights = scores.astype(BF16) * mask[b]
                o_ref[l, blk(b), hd(h)] = dot(weights, v_ref[l, blk(b), hd(h)], 1, 0)
        return carry

    lax.fori_loop(0, layers, inner, 0)

    def prepare(l, carry):
        for b in range(nb):
            qmt[l, :, blk(b)] = (q_ref[l, blk(b), :] * wide_mask(b, first[b])).T
            for h in range(heads):
                pt[l, h, b] = (
                    dot(k_ref[l, blk(b), hd(h)], q_ref[l, blk(b), hd(h)], 1, 1).astype(BF16) * maskt[b]
                )
        return carry

    lax.fori_loop(0, layers, prepare, 0)

    arrived(tabz.at[0 : nz - 1], tab_r)
    weights = owner_weights(0)
    for l in range(layers):
        owner(0, l, weights)

    before_chip = tabz[zmod(z - 1), 1:2, :]
    after_chip = tabz[zmod(z + 1), 0:1, :]
    before = jnp.where(is0, before_chip, last0)
    after = jnp.where(is0, first1, after_chip)
    prior = [before] + last[: nb - 1]
    later = first[1:] + [after]

    def select(l, carry):
        for b in range(nb):
            qs[l, blk(b), :] = q_ref[l, blk(b), :] * wide_mask(b, prior[b])
            seen_b = wide_mask(b, later[b])
            ks[l, blk(b), :] = k_ref[l, blk(b), :] * seen_b
            vs[l, blk(b), :] = v_ref[l, blk(b), :] * seen_b
        return carry

    lax.fori_loop(0, layers, select, 0)
    whole_loads[1].wait()
    store_ks.start()
    store_vs.start()
    small[1].wait()
    small[3].wait()
    for l in range(layers):
        gain8[l] = jnp.broadcast_to(gain_ref[l : l + 1, :], (8, heads * DH))
    joined = same(before_chip, last0)

    diagonal = lax.broadcasted_iota(jnp.int32, (128, 128), 0) == lax.broadcasted_iota(jnp.int32, (128, 128), 1)

    def carried(l):
        entered(0, l)
        for h in range(heads):
            state = dev[0, l, h]
            for b in range(nb):
                if b:
                    state = tails[l, h, b - 1] + same(prior[b - 1], prior[b]) * state
                cq[l, b, hd(h), hd(h)] = state.astype(BF16)
        tiles = [[], []]
        for b in range(nb):
            square, cross = None, None
            out = o_ref[l, blk(b), :] + dot(qs[l, blk(b), :], cq[l, b], 1, 0)
            o_ref[l, blk(b), :] = out
            for h in range(heads):
                o = out[:, hd(h)]
                a = g_ref[l, blk(b), hd(h)].astype(F32) * gain8[l, 0:1, hd(h)]
                square = o * o if square is None else square + o * o
                cross = a * o if cross is None else cross + a * o
            for n, x in enumerate((square, cross)):
                total = jnp.sum(x, axis=1, keepdims=True)
                for i in range(BLK // 128):
                    picked = jnp.where(diagonal, total[128 * i : 128 * (i + 1)], 0.0)
                    tiles[n].append(jnp.sum(picked, axis=0, keepdims=True))
        stat[l, f] = jnp.concatenate(tiles[0] + tiles[1], axis=0)
        for j in others:
            remote(stat.at[l, f], stat.at[l, f], st_s, st_r.at[l], fpeer(j)).start()

    for l in range(layers):
        entering(0, l, joined)
        if l > 0:
            carried(l - 1)
    carried(layers - 1)

    sent(mytile, tile_s)
    sent(tabz.at[0 : nz - 1], tab_s)
    sent_state(0)

    def gradient(l, carry):
        arrived(stat.at[l, 0 : nf - 1], st_r.at[l])
        summed = stat[l, 0]
        for i in range(1, nf):
            summed = summed + stat[l, i]
        r = lax.rsqrt(summed[0:8] / features + EPSILON)
        keep = keep_ref[l].astype(F32) / KEEP_RATE
        scale_a = keep * r
        scale_o = scale_a * (r * r) * (summed[8:16] / features)
        turned = jnp.concatenate([scale_a, scale_o, jnp.zeros((112, 128), F32)], axis=0).T
        gains = [jnp.zeros((1, DH), F32) for h in range(heads)]
        totals = [None] * heads
        for b in range(nb):
            per = BLK // 128
            col_a = jnp.concatenate(
                [jnp.broadcast_to(turned[:, per * b + i : per * b + i + 1], (128, 128)) for i in range(per)], axis=0
            )
            col_o = jnp.concatenate(
                [jnp.broadcast_to(turned[:, 8 + per * b + i : 9 + per * b + i], (128, 128)) for i in range(per)], axis=0
            )
            grads = []
            for h in range(heads):
                o = o_ref[l, blk(b), hd(h)]
                up = g_ref[l, blk(b), hd(h)].astype(F32) * col_a
                gains[h] = gains[h] + jnp.sum(up * o, axis=0, keepdims=True)
                grads.append((up * gain8[l, 0:1, hd(h)] - o * col_o).astype(BF16))
            grad = jnp.concatenate(grads, axis=1)
            do_ref[l, blk(b), :] = grad
            both = dot(qmt[l, :, blk(b)], grad, 1, 0)
            for h in range(heads):
                part = both[hd(h), hd(h)]
                fronts[l, h, b] = part
                part = part * same(first[b], first[0])
                totals[h] = part if totals[h] is None else totals[h] + part
        for h in range(heads):
            dsum[1, l, h] = totals[h]
            gain_sum[l, h] = jnp.broadcast_to(gains[h], (8, DH))
        hand_over(1, l)

        @pl.when(l > 0)
        def _():
            chip_total(1, l - 1, begin_own, begin_partner)

        return carry

    lax.fori_loop(0, layers, gradient, 0)
    for l in range(layers):
        for h in range(heads):
            gtile[heads * l + h : heads * l + h + 1, :] = gain_sum[l, h, 0:1, :]
    for i in range(heads * layers, 8):
        gtile[i : i + 1, :] = jnp.zeros((1, DH), F32)
    remote(gtile, gptile, gt_s, gt_r, partner).start()
    chip_total(1, layers - 1, begin_own, begin_partner)

    def outer_head(l, h):
        for b in range(nb):
            grad = do_ref[l, blk(b), hd(h)]
            v = v_ref[l, blk(b), hd(h)]
            vpart[l, blk(b), hd(h)] = dot(pt[l, h, b], grad, 1, 0)
            gst = dot(v, grad, 1, 1).astype(BF16) * maskt[b]
            kpart[l, blk(b), hd(h)] = dot(gst, q_ref[l, blk(b), hd(h)], 1, 0)

    def outer(l, carry):
        for h in range(heads):
            outer_head(l, h)
        return carry

    def outer_q(l, carry):
        for b in range(nb):
            carry_part = dot(do_ref[l, blk(b), :] * wide_mask(b, prior[b]), cq[l, b], 1, 1)
            for h in range(heads):
                gs = dot(do_ref[l, blk(b), hd(h)], v_ref[l, blk(b), hd(h)], 1, 1).astype(BF16) * mask[b]
                dq_ref[l, blk(b), hd(h)] = (
                    dot(gs, k_ref[l, blk(b), hd(h)], 1, 0) + carry_part[:, hd(h)]
                ).astype(BF16)
        return carry

    lax.fori_loop(0, layers - 2, outer, 0)
    outer_q(0, 0)
    arrived(gptile, gt_r)
    gslots[z] = gtile[...] + gptile[...]
    weights = owner_weights(1)
    for l in range(layers - 2):
        owner(1, l, weights)
    outer_head(layers - 2, 0)
    owner(1, layers - 2, weights)
    for h in range(1, heads):
        outer_head(layers - 2, h)
    owner(1, layers - 1, weights)
    for j in steps:
        remote(gslots.at[z], gslots.at[z], gz_s, gz_r, zpeer(j)).start()
    lax.fori_loop(layers - 1, layers, outer, 0)
    store_k.start()
    store_v.start()

    def later_states(l):
        entered(1, l)
        for h in range(heads):
            state = dev[1, l, h]
            for b in range(nb)[::-1]:
                if b < nb - 1:
                    state = fronts[l, h, b + 1] + same(later[b + 1], later[b]) * state
                rq_ref[l, h, b] = state.astype(BF16)
        pltpu.make_async_copy(rq_ref.at[l], rq_out.at[l], out_sem.at[5]).start()

    joined = same(after_chip, first1)
    for l in range(1, layers):
        outer_q(l, 0)
        entering(1, l - 1, joined)
    store_dq.start()
    sent(stat.at[:, 0 : nf - 1], st_s)
    sent(gtile, gt_s)

    for l in range(layers - 2):
        later_states(l)
    entering(1, layers - 1, joined)
    for l in range(max(0, layers - 2), layers):
        later_states(l)
    arrived(gslots.at[0 : nz - 1], gz_r)
    gtotal = gslots[0]
    for i in range(1, nz):
        gtotal = gtotal + gslots[i]
    for l in range(layers):
        for h in range(heads):
            gg_ref[l : l + 1, hd(h)] = gtotal[heads * l + h : heads * l + h + 1, :]
    small[2].start()
    sent(gslots.at[0 : nz - 1], gz_s)
    sent_state(1)
    for copy in (store_ks, store_vs, store_k, store_v, store_dq, small[2], store_rq):
        copy.wait()


def finish(
    layers, rows, heads,
    dq_ref, kpart, vpart, ks, vs, rq, gg_ref,
    dq_hbm, dk_hbm, dv_hbm, gg_hbm,
    dk_ref, dv_ref, sem, gg_sem,
):
    nb = rows // BLK
    gg_copy = pltpu.make_async_copy(gg_ref, gg_hbm, gg_sem)
    gg_copy.start()

    def copy(i, ref, hbm, l):
        return pltpu.make_async_copy(ref.at[l], hbm.at[l], sem.at[i, l])

    for l in range(layers):
        copy(0, dq_ref, dq_hbm, l).start()
    for l in range(layers):
        for b in range(nb):
            for h in range(heads):
                at = (l, slice(BLK * b, BLK * (b + 1)), slice(DH * h, DH * (h + 1)))
                dk_ref[at] = (kpart[at] + dot(vs[at], rq[l, h, b], 1, 1)).astype(BF16)
                dv_ref[at] = (vpart[at] + dot(ks[at], rq[l, h, b], 1, 0)).astype(BF16)
        copy(1, dk_ref, dk_hbm, l).start()
        copy(2, dv_ref, dv_hbm, l).start()
    gg_copy.wait()
    for l in range(layers):
        copy(0, dq_ref, dq_hbm, l).wait()
        copy(1, dk_ref, dk_hbm, l).wait()
        copy(2, dv_ref, dv_hbm, l).wait()


def local(queries, keys, values, out_grad, gain, keep_mask, segments):
    layers, rows, channels = queries.shape
    heads = channels // DH
    nz = lax.axis_size("seq") // 2
    nf = lax.axis_size("fsdp")
    nb = rows // BLK
    cut = DH // nz
    whole = (layers, rows, channels)
    vmem = pltpu.VMEM
    dma = pltpu.SemaphoreType.DMA
    hbm = pl.BlockSpec(memory_space=pl.ANY)

    def far(x):
        return pltpu.with_memory_space_constraint(x, pltpu.HBM)

    near = pl.BlockSpec(memory_space=pltpu.VMEM)
    scratch = [
        vmem(whole, BF16), vmem(whole, BF16), vmem(whole, BF16), vmem(whole, BF16), dma((layers,)), dma((2,)),
        vmem((layers, channels), F32), vmem((rows // 128, 128), jnp.int32),
        pltpu.SMEM((layers,), jnp.int32), dma((4,)), dma((6,)),
        vmem(whole, BF16), vmem((layers, heads, nb, DH, DH), BF16), vmem((layers, channels), F32),
        vmem((1, rows), F32), vmem((rows, 128), F32), vmem((nb, BLK, BLK), BF16), vmem((nb, BLK, BLK), BF16),
        vmem((8, 128), F32), vmem((8, 128), F32), vmem((nz, 2, 128), F32),
        vmem((layers, heads, nb, DH, DH), F32), vmem((layers, heads, nb, DH, DH), F32),
        vmem((layers, nb, channels, channels), BF16),
        vmem(whole, BF16), vmem((layers, channels, rows), BF16), vmem(whole, BF16), vmem(whole, BF16),
        vmem((layers, heads, nb, BLK, BLK), BF16),
        vmem(whole, F32), vmem(whole, BF16), vmem(whole, F32), vmem(whole, F32),
        vmem((2, layers, heads, DH, DH), F32), vmem((2, layers, DH, DH), F32), vmem((2, layers, DH, DH), F32),
        vmem((2, layers, nz, cut, DH), F32), vmem((2, layers, nz, cut, DH), F32),
        vmem((2, layers, DH, DH), F32), vmem((2, layers, DH, DH), F32), vmem((2, layers, heads, DH, DH), F32),
        vmem((layers, nf, 16, 128), F32), vmem((layers, 8, channels), F32), vmem((layers, heads, 8, DH), F32),
        vmem((8, 128), F32), vmem((8, 128), F32), vmem((nz, 8, 128), F32),
        dma, dma, dma, dma,
        dma, dma((2, layers)),
        dma, dma((2, layers)), dma((2, layers)),
        dma, dma((2, layers)),
        dma, dma((2, layers)),
        dma, dma((layers,)),
        dma, dma, dma, dma,
    ]
    results = pl.pallas_call(
        functools.partial(kernel, nz, nf, layers, rows, heads),
        out_shape=(
            vmem(whole, BF16),
            vmem(whole, F32),
            vmem(whole, F32),
            vmem(whole, BF16),
            vmem(whole, BF16),
            vmem((layers, heads, nb, DH, DH), BF16),
            vmem((layers, channels), F32),
        ),
        in_specs=[hbm] * 7,
        out_specs=(hbm,) * 7,
        scratch_shapes=scratch,
        compiler_params=pltpu.CompilerParams(
            collective_id=0, has_side_effects=True, vmem_limit_bytes=44 * 2**20
        ),
        name="backward",
    )(
        far(queries), far(keys), far(values), far(out_grad), far(gain), far(keep_mask),
        far(segments.reshape(rows // 128, 128)),
    )
    return pl.pallas_call(
        functools.partial(finish, layers, rows, heads),
        out_shape=(
            jax.ShapeDtypeStruct(whole, BF16),
            jax.ShapeDtypeStruct(whole, BF16),
            jax.ShapeDtypeStruct(whole, BF16),
            jax.ShapeDtypeStruct((layers, channels), F32),
        ),
        in_specs=[near] * 7,
        out_specs=(hbm,) * 4,
        scratch_shapes=[vmem(whole, BF16), vmem(whole, BF16), dma((3, layers)), dma],
        compiler_params=pltpu.CompilerParams(vmem_limit_bytes=8 * 2**20),
        name="finish",
    )(*[pltpu.with_memory_space_constraint(result, pltpu.VMEM) for result in results])


def solution(mesh):
    wide = P(None, "seq", "fsdp")
    in_specs = (wide, wide, wide, wide, P(None, "fsdp"), P(), P("seq"))
    out_specs = (wide, wide, wide, P(None, "fsdp"))
    return jax.shard_map(local, mesh=mesh, in_specs=in_specs, out_specs=out_specs, check_vma=False)
```
